32 devices in a mesh: wafer: 4 (over y, x), span: 8 (over z, core).
Axes of the slice: x: 2, y: 2, z: 4, core: 2. Of those that a mesh axis runs over, the one named last changes fastest.
Arguments:
- timestream: float32 [192, 2048], P(('wafer', 'span')), may hold values from -6 to 6
- templates: float32 [64, 2048], P(None, 'span'), may hold values from -0.125 to 0.125
- bias_group: int32 [192], P('wafer'), may hold values from 0 to 11, as said below
- det_weight: float32 [192], P('wafer'), may hold values from 0.2 to 5
- cut_start: int32 [192], P('wafer'), may hold values from 0 to 2047
- cut_len: int32 [192], P('wafer'), may hold values from 1 to 511
- pointing: int32 [192, 2048], P('wafer', 'span'), may hold values from 0 to 4095
- hit_tiles: int32 [8, 8], replicated, may hold values from 0 to 63, as said below
Outputs:
- fit_coeffs: float32 [192, 64], P(('wafer', 'span'))
- rhs_map: float32 [64, 512], P('span', 'wafer')
- weight_map: float32 [64, 512], P('span', 'wafer')
The draws below stay inside these ranges and needn't reach their ends.
Inputs may be any that keep to these rules, and one draw needn't show every extreme that they name: `bias_group`: within each wafer's 48 detectors every bias line holds exactly 4 detectors. `hit_tiles`: each row lists distinct tiles; tile t is owned by index t // 8 of span; every row holds exactly 2 tiles of each owner it names: of one owner common to all rows, and of 3 other owners.
All inputs are finite; a program needn't handle non-finite values.
Results may differ from the reference program's by a relative error of at most 0.0041.
Values sent between devices are 32-bit elements; how exact they have to be, the bound alone decides.
A program may use at most 64 MiB of HBM per device.

```python
import math
import jax
import jax.numpy as jnp
from jax import lax

TCH = 256
NT = 64
NGROUP = 12
TILE = 512
TILE_OWN = 8
CAP = 2
DET_W = 48
DET = 192
SAMP = 2048
HIT = 8
NTILE = 64


def draw_bias_group(key, part):
    wafers = DET // DET_W

    def one_wafer(wafer_index):
        order = jax.random.permutation(jax.random.fold_in(key, wafer_index), DET_W)
        return (order % NGROUP).astype(jnp.int32)
    return jax.vmap(one_wafer)(jnp.arange(wafers, dtype=jnp.int32)).reshape(DET)


def draw_hit_tiles(key, part):
    owner_count = NTILE // TILE_OWN
    other_count = HIT // CAP - 1
    center = jax.random.randint(jax.random.fold_in(key, 7), (), 0, owner_count)

    def one_span(span_index):
        span_key = jax.random.fold_in(key, 1000 + span_index)
        scores = jax.random.randint(jax.random.fold_in(span_key, 1), (owner_count - 1,), 0, 2 ** 30)
        others = jnp.argsort(scores, stable=True)[:other_count].astype(jnp.int32)
        others = others + (others >= center).astype(jnp.int32)
        tile_scores = jax.random.randint(jax.random.fold_in(span_key, 2), (other_count, TILE_OWN), 0, 2 ** 30)
        within = jnp.argsort(tile_scores, axis=1, stable=True)[:, :CAP].astype(jnp.int32)
        central = center * TILE_OWN + TILE_OWN - CAP + jnp.arange(CAP, dtype=jnp.int32)
        spread = (others[:, None] * TILE_OWN + within).reshape(-1)
        listed = jnp.concatenate([central, spread])
        order = jax.random.permutation(jax.random.fold_in(span_key, 3), HIT)
        return listed[order].astype(jnp.int32)
    return jax.vmap(one_span)(jnp.arange(owner_count, dtype=jnp.int32))


def with_ends(values, rng, smallest, high):
    shape = values.shape
    spot = [jax.random.randint(jax.random.fold_in(rng, axis), (), 0, shape[axis]) for axis in range(len(shape))]
    values = values.at[tuple(spot)].set(smallest)
    longest = shape.index(max(shape))
    spot[longest] = (spot[longest] + 1) % shape[longest]
    return values.at[tuple(spot)].set(high)


def levels(own_key, shape, shards, smallest, high):
    factor_of, own = 1.0, jax.random.fold_in(own_key, 6)
    for dim, parts in shards:
        steps = jnp.exp(jax.random.uniform(jax.random.fold_in(own, dim), (parts,), jnp.float32, smallest / len(shards), high / len(shards)))
        factor_of = factor_of * jnp.repeat(steps, shape[dim] // parts).reshape([-1 if axis == dim else 1 for axis in range(len(shape))])
    return factor_of


def noise(key, shape, scale, most, pieces=(), held_as=jnp.bfloat16):
    factor_of = levels(key, shape, pieces, -0.22, 0.18) if pieces else 1.0
    drawn = jax.random.normal(key, shape, jnp.float32) * scale * factor_of
    return jnp.minimum(jnp.maximum(drawn, -most), most).astype(held_as)


def setup_inputs(seed: int = 0) -> dict:
    arg_keys = jax.random.split(jax.random.key(seed), 9)
    timestream = noise(arg_keys[0], (DET, SAMP), 1.0, 6.0, ((0, 32),), jnp.float32)
    templates = noise(arg_keys[1], (NT, SAMP), SAMP ** -0.5, 0.125, ((1, 8),), jnp.float32)
    bias_group = draw_bias_group(jax.random.fold_in(arg_keys[8], 71), 0)
    det_weight = jnp.clip(jnp.exp(math.log(5.0) - 3.218876 * jax.random.uniform(arg_keys[3], (DET,), jnp.float32) ** levels(arg_keys[3], (DET,), ((0, 4),), -0.2, 0.2)), 0.2, 5.0)
    cut_start = with_ends(jax.random.randint(arg_keys[4], (DET,), 0, SAMP), jax.random.fold_in(arg_keys[4], 1), 0, SAMP - 1).astype(jnp.int32)
    cut_len = with_ends(jax.random.randint(arg_keys[5], (DET,), 1, 2 * TCH), jax.random.fold_in(arg_keys[5], 1), 1, (2 * TCH) - 1).astype(jnp.int32)
    pointing = with_ends(jax.random.randint(arg_keys[6], (DET, SAMP), 0, HIT * TILE), jax.random.fold_in(arg_keys[6], 1), 0, (HIT * TILE) - 1).astype(jnp.int32)
    hit_tiles = draw_hit_tiles(jax.random.fold_in(arg_keys[8], 71), 0)
    return {"timestream": timestream, "templates": templates, "bias_group": bias_group, "det_weight": det_weight, "cut_start": cut_start, "cut_len": cut_len, "pointing": pointing, "hit_tiles": hit_tiles}


def solve_normal(matrix, right_side):
    factor = jnp.linalg.cholesky(matrix)
    middle = lax.linalg.triangular_solve(factor, right_side, left_side=True, lower=True)
    return lax.linalg.triangular_solve(factor, middle, left_side=True, lower=True, transpose_a=True)

def reference(timestream, templates, bias_group, det_weight, cut_start, cut_len, pointing, hit_tiles):
    highest = lax.Precision.HIGHEST
    wafers = DET // DET_W
    by_wafer = timestream.reshape(wafers, DET_W, SAMP)
    wafer_groups = bias_group.reshape(wafers, DET_W)
    onehot = (wafer_groups[:, None, :] == jnp.arange(NGROUP, dtype=jnp.int32)[None, :, None]).astype(jnp.float32)
    line_mean = jnp.einsum('wgd,wds->wgs', onehot, by_wafer, precision=highest) * (NGROUP / DET_W)
    common = jnp.einsum('wgd,wgs->wds', onehot, line_mean, precision=highest)
    cleaned = (by_wafer - common).reshape(DET, SAMP)
    gram = jnp.dot(templates.astype(jnp.float32), templates.T.astype(jnp.float32), precision=highest, preferred_element_type=jnp.float32)
    projection = jnp.dot(templates.astype(jnp.float32), cleaned.T.astype(jnp.float32), precision=highest, preferred_element_type=jnp.float32)
    amplitudes = solve_normal(gram, projection)
    filtered = cleaned - jnp.dot(amplitudes.T.astype(jnp.float32), templates.astype(jnp.float32), precision=highest, preferred_element_type=jnp.float32)
    sample_time = jnp.arange(SAMP, dtype=jnp.int32)
    inside = (sample_time[None, :] >= cut_start[:, None]) & (sample_time[None, :] < (cut_start + cut_len)[:, None])
    sample_weight = jnp.where(inside, jnp.float32(0.0), det_weight[:, None]).astype(jnp.bfloat16)
    weighted = (sample_weight.astype(jnp.float32) * filtered).astype(jnp.bfloat16)
    span_of = sample_time // TCH
    tile_index = hit_tiles[span_of[None, :], pointing // TILE]
    pixel = (tile_index * TILE + pointing % TILE).astype(jnp.int32).reshape(-1)
    rhs_map = jax.ops.segment_sum(weighted.astype(jnp.float32).reshape(-1), pixel, num_segments=NTILE * TILE)
    weight_map = jax.ops.segment_sum(sample_weight.astype(jnp.float32).reshape(-1), pixel, num_segments=NTILE * TILE)
    return (amplitudes.T, rhs_map.reshape(NTILE, TILE), weight_map.reshape(NTILE, TILE))
```

```python
import functools

import jax
import jax.numpy as jnp
from jax import lax
from jax.experimental import pallas as pl
from jax.experimental.pallas import tpu as pltpu
from jax.sharding import PartitionSpec as P

NGROUP = 12
TILE = 512
TILE_OWN = 8
CAP = 2
ROWS = 8
HIGHEST = lax.Precision.HIGHEST
MESH = pl.DeviceIdType.MESH
F32 = jnp.float32
BF16 = jnp.bfloat16


def dot_nn(a, b):
    return lax.dot_general(a, b, (((1,), (0,)), ((), ())), precision=HIGHEST, preferred_element_type=F32)


def dot_nt(a, b):
    return lax.dot_general(a, b, (((1,), (1,)), ((), ())), precision=HIGHEST, preferred_element_type=F32)


def dot_tn(a, b):
    return lax.dot_general(a, b, (((0,), (0,)), ((), ())), precision=HIGHEST, preferred_element_type=F32)


def iota(shape, dim):
    return lax.broadcasted_iota(jnp.int32, shape, dim)


def to_column(row):
    size = row.shape[1]
    eye = iota((size, size), 0) == iota((size, size), 1)
    return jnp.sum(jnp.where(eye, row.astype(F32), 0.0), axis=1, keepdims=True)


def log2(value):
    assert value & (value - 1) == 0
    return value.bit_length() - 1


def inverse_spd(gram):
    size = gram.shape[0]
    eye = (iota((size, size), 0) == iota((size, size), 1)).astype(F32)
    wide = jnp.concatenate([eye, gram], axis=1)
    blocks = [wide[ROWS * b : ROWS * (b + 1), :] for b in range(size // ROWS)]
    below = iota((ROWS, 1), 0)
    for k in range(size):
        first, r = k // ROWS, k % ROWS
        row = blocks[first][r : r + 1, :]
        scaled = row * (1.0 / row[:, size + k : size + k + 1])
        for b in range(first, len(blocks)):
            if b == first and r == ROWS - 1:
                continue
            column = blocks[b][:, size + k : size + k + 1]
            if b == first:
                column = jnp.where(below > r, column, 0.0)
            blocks[b] = blocks[b] - column * scaled
    done = jnp.concatenate(blocks, axis=0)
    on_diag = iota(done.shape, 0) + size == iota(done.shape, 1)
    pivots = jnp.sum(jnp.where(on_diag, done, 0.0), axis=1, keepdims=True)
    lower = done[:, :size]
    return dot_tn(lower, lower / pivots)


def kernel(
    wafers, spans,
    ts_ref, tm_ref, bg_ref, dw_ref, cs_ref, cl_ref, pt_ref, ht_ref,
    fit_ref, rhs_ref, wgt_ref,
    ts_rx, ts_all, gr_rx, pj_rx, sw_ref, val_ref, hot_ref, tx, rx,
    span_send, span_recv, tile_send, tile_recv,
):
    det_dev = ts_ref.shape[0]
    nt, span_len = tm_ref.shape
    det_w = pt_ref.shape[0]
    hits = ht_ref.shape[1]
    total = wafers * spans
    pix = TILE // wafers
    my_w, my_s = lax.axis_index("wafer"), lax.axis_index("span")
    me = my_w * spans + my_s

    def peer(i):
        other = lax.rem(me + i, total)
        return other, lax.div(other, spans), lax.rem(other, spans)

    barrier = pltpu.get_barrier_semaphore()

    def greet(i, carry):
        unused, w, s = peer(i)
        pl.semaphore_signal(barrier, inc=1, device_id=(w, s), device_id_type=MESH)
        return carry

    lax.fori_loop(1, total, greet, 0)

    templates = tm_ref[...]
    gr_rx[my_s] = dot_nt(templates, templates)
    ts_rx[my_s] = ts_ref[:, pl.ds(pl.multiple_of(my_s * span_len, span_len), span_len)]
    pl.semaphore_wait(barrier, total - 1)

    def to_span(src, dst, which, s):
        pltpu.make_async_remote_copy(
            src_ref=src, dst_ref=dst, send_sem=span_send.at[which], recv_sem=span_recv.at[which],
            device_id=(my_w, s), device_id_type=MESH,
        ).start()

    def span_wait(buffer, sems, which):
        slots = buffer.at[pl.ds(0, spans - 1)]
        pltpu.make_async_copy(slots, slots, sems.at[which]).wait()

    others = [lax.rem(my_s + i, spans) for i in range(1, spans)]
    for s in others:
        start = pl.multiple_of(s * span_len, span_len)
        to_span(ts_ref.at[:, pl.ds(start, span_len)], ts_rx.at[my_s], 0, s)
    for s in others:
        to_span(gr_rx.at[my_s], gr_rx.at[my_s], 1, s)

    listed = ht_ref[...]
    owner = lax.shift_right_logical(listed, jnp.full(listed.shape, log2(TILE_OWN), jnp.int32)).astype(F32)
    lane = iota(listed.shape, 1)
    rank = jnp.zeros(listed.shape, F32)
    for j in range(hits - 1):
        rank += jnp.where((owner[:, j : j + 1] == owner) & (lane > j), 1.0, 0.0)
    code = owner * CAP + rank
    own_code = jnp.sum(jnp.where(iota(listed.shape, 0) == my_s, code, 0.0), axis=0, keepdims=True)
    slots = spans * CAP
    selector = (own_code == iota((slots, hits), 0).astype(F32)).astype(F32)
    landing = []
    for k in range(CAP):
        mine = code == (my_s * CAP + k).astype(F32)
        place = (listed - (my_s * TILE_OWN - 1)).astype(F32)
        landing.append(jnp.sum(jnp.where(mine, place, 0.0), axis=1, keepdims=True) - 1.0)

    time = (iota((det_w, span_len), 1) + my_s * span_len).astype(F32)
    cut_start = to_column(cs_ref[...])
    cut_end = cut_start + to_column(cl_ref[...])
    inside = (time >= cut_start) & (time < cut_end)
    sw_ref[...] = jnp.where(inside, 0.0, to_column(dw_ref[...])).astype(BF16).astype(F32)

    coarse_count = wafers * hits
    coarse_iota = iota((coarse_count, span_len), 0)
    fine_iota = iota((pix, span_len), 0)

    def shifted(x, amount):
        return lax.shift_right_logical(x, jnp.full(x.shape, amount, jnp.int32))

    def coarse_of(points):
        return (shifted(points, log2(pix)) & (wafers - 1)) * hits + shifted(points, log2(TILE))

    def bin_rows(source, first_time):
        def step(g, acc):
            rows = pl.ds(pl.multiple_of(g * ROWS, ROWS), ROWS)
            points = pt_ref[rows, :]
            coarse = coarse_of(points)
            fine = points & (pix - 1)
            values = source[rows, :]
            for r in range(ROWS):
                left = jnp.where(coarse_iota == coarse[r : r + 1, :], values[r : r + 1, :], 0.0).astype(BF16)
                if first_time:
                    right = jnp.where(fine_iota == fine[r : r + 1, :], 1.0, 0.0).astype(BF16)
                    hot_ref[g * ROWS + r] = right
                else:
                    right = hot_ref[g * ROWS + r]
                acc = acc + lax.dot_general(
                    left, right, (((1,), (1,)), ((), ())), preferred_element_type=F32
                )
            return acc

        return lax.fori_loop(0, det_w // ROWS, step, jnp.zeros((coarse_count, pix), F32))

    def send_tiles(part, m):
        wide = jnp.concatenate([part[q * hits : (q + 1) * hits, :] for q in range(wafers)], axis=1)
        out = dot_nn(selector, wide)
        for q in range(wafers):
            for o in range(spans):
                tx[m, q * spans + o] = out[o * CAP : (o + 1) * CAP, q * pix : (q + 1) * pix]
        rx[m, me] = tx[m, me]

        def send(i, carry):
            other, w, s = peer(i)
            pltpu.make_async_remote_copy(
                src_ref=tx.at[m, other], dst_ref=rx.at[m, me],
                send_sem=tile_send.at[m], recv_sem=tile_recv.at[m],
                device_id=(w, s), device_id_type=MESH,
            ).start()
            return carry

        lax.fori_loop(1, total, send, 0)

    def tile_wait(buffer, sems, m):
        part = buffer.at[m, pl.ds(0, total - 1)]
        pltpu.make_async_copy(part, part, sems.at[m]).wait()

    def collect(m):
        row_iota = iota((TILE_OWN, pix), 0).astype(F32)
        acc = jnp.zeros((TILE_OWN, pix), F32)
        for s in range(spans):
            arrived = rx[m, s]
            for w in range(1, wafers):
                arrived = arrived + rx[m, w * spans + s]
            for k in range(CAP):
                acc = acc + jnp.where(row_iota == landing[k][s : s + 1, :], arrived[k : k + 1, :], 0.0)
        return acc

    send_tiles(bin_rows(sw_ref, True), 1)

    same_line = (bg_ref[...].astype(F32) == to_column(bg_ref[...])).astype(F32)
    span_wait(ts_rx, span_recv, 0)
    for s in range(spans):
        ts_all[s * det_dev : (s + 1) * det_dev, :] = ts_rx[s]
    stream = ts_all[...]
    cleaned = stream - dot_nn(same_line, stream) * (NGROUP / det_w)
    pj_rx[my_s] = dot_nt(cleaned, templates)
    for s in others:
        to_span(pj_rx.at[my_s], pj_rx.at[my_s], 2, s)

    span_wait(gr_rx, span_recv, 1)
    inverse = inverse_spd(jnp.sum(gr_rx[...], axis=0))
    solved = dot_nn(inverse, templates)

    span_wait(pj_rx, span_recv, 2)
    projection = jnp.sum(pj_rx[...], axis=0)
    filtered = cleaned - dot_nn(projection, solved)
    val_ref[...] = (sw_ref[...] * filtered).astype(BF16).astype(F32)
    send_tiles(bin_rows(val_ref, False), 0)

    mine = (iota((det_dev, det_w), 1) == iota((det_dev, det_w), 0) + my_s * det_dev).astype(F32)
    fit_ref[...] = dot_nn(dot_nn(mine, projection), inverse)
    tile_wait(rx, tile_recv, 1)
    wgt_ref[...] = collect(1)
    tile_wait(rx, tile_recv, 0)
    rhs_ref[...] = collect(0)
    for which, buffer in enumerate((ts_rx, gr_rx, pj_rx)):
        span_wait(buffer, span_send, which)
    for m in range(2):
        tile_wait(tx, tile_send, m)


def body(timestream, templates, bias_group, det_weight, cut_start, cut_len, pointing, hit_tiles):
    wafers, spans = lax.axis_size("wafer"), lax.axis_size("span")
    det_dev = timestream.shape[0]
    nt, span_len = templates.shape
    det_w = pointing.shape[0]
    pix = TILE // wafers
    total = wafers * spans
    vmem = pl.BlockSpec(memory_space=pltpu.VMEM)
    return pl.pallas_call(
        functools.partial(kernel, wafers, spans),
        out_shape=(
            jax.ShapeDtypeStruct((det_dev, nt), F32),
            jax.ShapeDtypeStruct((TILE_OWN, pix), F32),
            jax.ShapeDtypeStruct((TILE_OWN, pix), F32),
        ),
        in_specs=[vmem] * 8,
        out_specs=(vmem,) * 3,
        scratch_shapes=[
            pltpu.VMEM((spans, det_dev, span_len), F32),
            pltpu.VMEM((det_w, span_len), F32),
            pltpu.VMEM((spans, nt, nt), F32),
            pltpu.VMEM((spans, det_w, nt), F32),
            pltpu.VMEM((det_w, span_len), F32),
            pltpu.VMEM((det_w, span_len), F32),
            pltpu.VMEM((det_w, pix, span_len), BF16),
            pltpu.VMEM((2, total, CAP, pix), F32),
            pltpu.VMEM((2, total, CAP, pix), F32),
            pltpu.SemaphoreType.DMA((3,)),
            pltpu.SemaphoreType.DMA((3,)),
            pltpu.SemaphoreType.DMA((2,)),
            pltpu.SemaphoreType.DMA((2,)),
        ],
        compiler_params=pltpu.CompilerParams(
            collective_id=0, has_side_effects=True, vmem_limit_bytes=56 * 1024 * 1024
        ),
    )(
        timestream, templates, bias_group.reshape(1, det_w), det_weight.reshape(1, det_w),
        cut_start.reshape(1, det_w), cut_len.reshape(1, det_w), pointing, hit_tiles,
    )


def solution(mesh):
    in_specs = (
        P(("wafer", "span"), None),
        P(None, "span"),
        P("wafer"),
        P("wafer"),
        P("wafer"),
        P("wafer"),
        P("wafer", "span"),
        P(),
    )
    out_specs = (P(("wafer", "span"), None), P("span", "wafer"), P("span", "wafer"))
    return jax.shard_map(body, mesh=mesh, in_specs=in_specs, out_specs=out_specs, check_vma=False)
```

```python
import functools

import jax
import jax.numpy as jnp
from jax import lax
from jax.experimental import pallas as pl
from jax.experimental.pallas import tpu as pltpu
from jax.sharding import PartitionSpec as P

NGROUP = 12
TILE = 512
TILE_OWN = 8
CAP = 2
ROWS = 8
HIGHEST = lax.Precision.HIGHEST
MESH = pl.DeviceIdType.MESH
F32 = jnp.float32
BF16 = jnp.bfloat16


def dot_nn(a, b):
    return lax.dot_general(a, b, (((1,), (0,)), ((), ())), precision=HIGHEST, preferred_element_type=F32)


def dot_nt(a, b):
    return lax.dot_general(a, b, (((1,), (1,)), ((), ())), precision=HIGHEST, preferred_element_type=F32)


def dot_tn(a, b):
    return lax.dot_general(a, b, (((0,), (0,)), ((), ())), precision=HIGHEST, preferred_element_type=F32)


def iota(shape, dim):
    return lax.broadcasted_iota(jnp.int32, shape, dim)


def to_column(row):
    size = row.shape[1]
    eye = iota((size, size), 0) == iota((size, size), 1)
    return jnp.sum(jnp.where(eye, row.astype(F32), 0.0), axis=1, keepdims=True)


def log2(value):
    assert value & (value - 1) == 0
    return value.bit_length() - 1


def inverse_spd(gram):
    size = gram.shape[0]
    wide = 2 * size
    eye = (iota((size, size), 0) == iota((size, size), 1)).astype(F32)
    joined = jnp.concatenate([eye, gram], axis=1)
    blocks = [joined[ROWS * b : ROWS * (b + 1), :] for b in range(size // ROWS)]
    row_of = iota((ROWS, wide), 0)
    for p in range(size // ROWS):
        spread = [
            [
                jnp.broadcast_to(block[:, size + p * ROWS + c : size + p * ROWS + c + 1], (ROWS, wide))
                for c in range(ROWS)
            ]
            for block in blocks
        ]
        panel = blocks[p]
        columns = list(spread[p])
        for k in range(ROWS):
            pivot = columns[k]
            scale = 1.0 / pivot[k : k + 1, :]
            here = row_of == k
            top = panel[k : k + 1, :] * scale
            panel = jnp.where(here, top, panel - pivot * top)
            for c in range(k + 1, ROWS):
                top = columns[c][k : k + 1, :] * scale
                columns[c] = jnp.where(here, top, columns[c] - pivot * top)
        for b in range(len(blocks)):
            if b == p:
                blocks[b] = panel
            else:
                terms = [spread[b][c] * panel[c : c + 1, :] for c in range(ROWS)]
                while len(terms) > 1:
                    terms = [x + y for x, y in zip(terms[::2], terms[1::2])]
                blocks[b] = blocks[b] - terms[0]
    return jnp.concatenate(blocks, axis=0)[:, :size]


def kernel(
    wafers, spans,
    ts_ref, tm_hbm, bg_hbm, dw_hbm, cs_hbm, cl_hbm, pt_hbm, ht_hbm,
    fit_ref, rhs_ref, wgt_ref,
    tm_ref, bg_ref, dw_ref, cs_ref, cl_ref, pt_ref, ht_ref,
    ts_rx, ts_all, gr_rx, pj_rx, sw_ref, val_ref, hot_ref, tx, rx,
    span_send, span_recv, tile_send, tile_recv, local_sem,
):
    det_dev = ts_ref.shape[0]
    nt, span_len = tm_ref.shape
    det_w = pt_ref.shape[0]
    hits = ht_ref.shape[1]
    total = wafers * spans
    pix = TILE // wafers
    my_w, my_s = lax.axis_index("wafer"), lax.axis_index("span")
    me = my_w * spans + my_s

    s_peers = [lax.rem(my_s + i, spans) for i in range(spans)]
    w_peers = [lax.rem(my_w + i, wafers) for i in range(wafers)]
    others = s_peers[1:]

    def for_peers(act):
        if total <= 64:
            for s in range(spans):
                for w in range(wafers):
                    if w or s:
                        act(w_peers[w], s_peers[s])
        else:

            def step(i, carry):
                other = lax.rem(me + i, total)
                act(lax.div(other, spans), lax.rem(other, spans))
                return carry

            lax.fori_loop(1, total, step, 0)

    def own_start(s):
        return pl.multiple_of(s * span_len, span_len)

    pairs = (
        (tm_hbm, tm_ref),
        (ts_ref.at[:, pl.ds(own_start(my_s), span_len)], ts_rx.at[my_s]),
        (pt_hbm, pt_ref), (cs_hbm, cs_ref), (cl_hbm, cl_ref), (dw_hbm, dw_ref), (ht_hbm, ht_ref), (bg_hbm, bg_ref),
    )
    local = [pltpu.make_async_copy(a, b, local_sem.at[i]) for i, (a, b) in enumerate(pairs)]
    for copy in local:
        copy.start()
    barrier = pltpu.get_barrier_semaphore()
    for_peers(
        lambda w, s: pl.semaphore_signal(barrier, inc=1, device_id=(w, s), device_id_type=MESH)
    )
    local[0].wait()
    templates = tm_ref[...]
    gr_rx[my_s] = dot_nt(templates, templates)
    pl.semaphore_wait(barrier, total - 1)

    def to_span(src, dst, which, s):
        pltpu.make_async_remote_copy(
            src_ref=src, dst_ref=dst, send_sem=span_send.at[which], recv_sem=span_recv.at[which],
            device_id=(my_w, s), device_id_type=MESH,
        ).start()

    def span_wait(buffer, sems, which):
        slots = buffer.at[pl.ds(0, spans - 1)]
        pltpu.make_async_copy(slots, slots, sems.at[which]).wait()

    for s in others:
        to_span(ts_ref.at[:, pl.ds(own_start(s), span_len)], ts_rx.at[my_s], 0, s)
    for s in others:
        to_span(gr_rx.at[my_s], gr_rx.at[my_s], 1, s)

    for copy in local[2:]:
        copy.wait()

    listed = ht_ref[...]
    owner = lax.shift_right_logical(listed, jnp.full(listed.shape, log2(TILE_OWN), jnp.int32)).astype(F32)
    lane = iota(listed.shape, 1)
    rank = jnp.zeros(listed.shape, F32)
    for j in range(hits - 1):
        rank += jnp.where((owner[:, j : j + 1] == owner) & (lane > j), 1.0, 0.0)
    code = owner * CAP + rank
    own_code = jnp.sum(jnp.where(iota(listed.shape, 0) == my_s, code, 0.0), axis=0, keepdims=True)
    slots = spans * CAP
    selector = (own_code == iota((slots, hits), 0).astype(F32)).astype(F32)
    landing = []
    for k in range(CAP):
        mine = code == (my_s * CAP + k).astype(F32)
        place = (listed - (my_s * TILE_OWN - 1)).astype(F32)
        landing.append(jnp.sum(jnp.where(mine, place, 0.0), axis=1, keepdims=True) - 1.0)

    time = (iota((det_w, span_len), 1) + my_s * span_len).astype(F32)
    cut_start = to_column(cs_ref[...])
    cut_end = cut_start + to_column(cl_ref[...])
    inside = (time >= cut_start) & (time < cut_end)
    sw_ref[...] = jnp.where(inside, 0.0, to_column(dw_ref[...])).astype(BF16).astype(F32)

    coarse_count = wafers * hits
    coarse_iota = iota((coarse_count, span_len), 0)
    fine_iota = iota((pix, span_len), 0)

    def shifted(x, amount):
        return lax.shift_right_logical(x, jnp.full(x.shape, amount, jnp.int32))

    def coarse_of(points):
        return (shifted(points, log2(pix)) & (wafers - 1)) * hits + shifted(points, log2(TILE))

    def bin_rows(source, first_time):
        def step(g, acc):
            rows = pl.ds(pl.multiple_of(g * ROWS, ROWS), ROWS)
            points = pt_ref[rows, :]
            coarse = coarse_of(points)
            fine = points & (pix - 1)
            values = source[rows, :]
            left = jnp.concatenate(
                [
                    jnp.where(coarse_iota == coarse[r : r + 1, :], values[r : r + 1, :], 0.0).astype(BF16)
                    for r in range(ROWS)
                ],
                axis=1,
            )
            if first_time:
                right = jnp.concatenate(
                    [
                        jnp.where(fine_iota == fine[r : r + 1, :], 1.0, 0.0).astype(BF16)
                        for r in range(ROWS)
                    ],
                    axis=1,
                )
                hot_ref[g] = right
            else:
                right = hot_ref[g]
            return acc + lax.dot_general(
                left, right, (((1,), (1,)), ((), ())), preferred_element_type=F32
            )

        return lax.fori_loop(0, det_w // ROWS, step, jnp.zeros((coarse_count, pix), F32), unroll=2)

    def send_tiles(part, m):
        wide = jnp.concatenate([part[q * hits : (q + 1) * hits, :] for q in range(wafers)], axis=1)
        out = dot_nn(selector, wide)
        for q in range(wafers):
            for o in range(spans):
                tx[m, q * spans + o] = out[o * CAP : (o + 1) * CAP, q * pix : (q + 1) * pix]
        rx[m, me] = tx[m, me]

        def send(w, s):
            pltpu.make_async_remote_copy(
                src_ref=tx.at[m, w * spans + s], dst_ref=rx.at[m, me],
                send_sem=tile_send.at[m], recv_sem=tile_recv.at[m],
                device_id=(w, s), device_id_type=MESH,
            ).start()

        for_peers(send)

    def tile_wait(buffer, sems, m):
        part = buffer.at[m, pl.ds(0, total - 1)]
        pltpu.make_async_copy(part, part, sems.at[m]).wait()

    def collect(m):
        row_iota = iota((TILE_OWN, pix), 0).astype(F32)
        acc = jnp.zeros((TILE_OWN, pix), F32)
        for s in range(spans):
            arrived = rx[m, s]
            for w in range(1, wafers):
                arrived = arrived + rx[m, w * spans + s]
            for k in range(CAP):
                acc = acc + jnp.where(row_iota == landing[k][s : s + 1, :], arrived[k : k + 1, :], 0.0)
        return acc

    send_tiles(bin_rows(sw_ref, True), 1)

    same_line = (bg_ref[...].astype(F32) == to_column(bg_ref[...])).astype(F32)
    local[1].wait()
    span_wait(ts_rx, span_recv, 0)
    for s in range(spans):
        ts_all[s * det_dev : (s + 1) * det_dev, :] = ts_rx[s]
    stream = ts_all[...]
    cleaned = stream - dot_nn(same_line, stream) * (NGROUP / det_w)
    pj_rx[my_s] = dot_nt(cleaned, templates)
    for s in others:
        to_span(pj_rx.at[my_s], pj_rx.at[my_s], 2, s)

    span_wait(gr_rx, span_recv, 1)
    inverse = inverse_spd(jnp.sum(gr_rx[...], axis=0))
    solved = dot_nn(inverse, templates)

    span_wait(pj_rx, span_recv, 2)
    projection = jnp.sum(pj_rx[...], axis=0)
    filtered = cleaned - dot_nn(projection, solved)
    val_ref[...] = (sw_ref[...] * filtered).astype(BF16).astype(F32)
    send_tiles(bin_rows(val_ref, False), 0)

    mine = (iota((det_dev, det_w), 1) == iota((det_dev, det_w), 0) + my_s * det_dev).astype(F32)
    fit_ref[...] = dot_nn(dot_nn(mine, projection), inverse)
    tile_wait(rx, tile_recv, 1)
    wgt_ref[...] = collect(1)
    tile_wait(rx, tile_recv, 0)
    rhs_ref[...] = collect(0)
    for which, buffer in enumerate((ts_rx, gr_rx, pj_rx)):
        span_wait(buffer, span_send, which)
    for m in range(2):
        tile_wait(tx, tile_send, m)


def hand_on(*refs):
    sems = refs[6]
    copies = [pltpu.make_async_copy(refs[i], refs[3 + i], sems.at[i]) for i in range(3)]
    for copy in copies:
        copy.start()
    for copy in copies:
        copy.wait()


def body(timestream, templates, bias_group, det_weight, cut_start, cut_len, pointing, hit_tiles):
    wafers, spans = lax.axis_size("wafer"), lax.axis_size("span")
    det_dev = timestream.shape[0]
    nt, span_len = templates.shape
    det_w = pointing.shape[0]
    pix = TILE // wafers
    total = wafers * spans
    vmem = pl.BlockSpec(memory_space=pltpu.VMEM)
    results = (
        jax.ShapeDtypeStruct((det_dev, nt), F32),
        jax.ShapeDtypeStruct((TILE_OWN, pix), F32),
        jax.ShapeDtypeStruct((TILE_OWN, pix), F32),
    )
    outs = pl.pallas_call(
        functools.partial(kernel, wafers, spans),
        out_shape=results,
        in_specs=[pl.BlockSpec(memory_space=pl.ANY)] * 8,
        out_specs=(vmem,) * 3,
        scratch_shapes=[
            pltpu.VMEM((nt, span_len), F32),
            pltpu.VMEM((1, det_w), jnp.int32),
            pltpu.VMEM((1, det_w), F32),
            pltpu.VMEM((1, det_w), jnp.int32),
            pltpu.VMEM((1, det_w), jnp.int32),
            pltpu.VMEM((det_w, span_len), jnp.int32),
            pltpu.VMEM(hit_tiles.shape, jnp.int32),
            pltpu.VMEM((spans, det_dev, span_len), F32),
            pltpu.VMEM((det_w, span_len), F32),
            pltpu.VMEM((spans, nt, nt), F32),
            pltpu.VMEM((spans, det_w, nt), F32),
            pltpu.VMEM((det_w, span_len), F32),
            pltpu.VMEM((det_w, span_len), F32),
            pltpu.VMEM((det_w // ROWS, pix, ROWS * span_len), BF16),
            pltpu.VMEM((2, total, CAP, pix), F32),
            pltpu.VMEM((2, total, CAP, pix), F32),
            pltpu.SemaphoreType.DMA((3,)),
            pltpu.SemaphoreType.DMA((3,)),
            pltpu.SemaphoreType.DMA((2,)),
            pltpu.SemaphoreType.DMA((2,)),
            pltpu.SemaphoreType.DMA((8,)),
        ],
        compiler_params=pltpu.CompilerParams(
            collective_id=0, has_side_effects=True, vmem_limit_bytes=56 * 1024 * 1024
        ),
    )(
        timestream, templates, bias_group.reshape(1, det_w), det_weight.reshape(1, det_w),
        cut_start.reshape(1, det_w), cut_len.reshape(1, det_w), pointing, hit_tiles,
    )
    anywhere = pl.BlockSpec(memory_space=pl.ANY)
    return pl.pallas_call(
        hand_on,
        out_shape=results,
        in_specs=[anywhere] * 3,
        out_specs=(anywhere,) * 3,
        scratch_shapes=[pltpu.SemaphoreType.DMA((3,))],
    )(*outs)


def solution(mesh):
    in_specs = (
        P(("wafer", "span"), None),
        P(None, "span"),
        P("wafer"),
        P("wafer"),
        P("wafer"),
        P("wafer"),
        P("wafer", "span"),
        P(),
    )
    out_specs = (P(("wafer", "span"), None), P("span", "wafer"), P("span", "wafer"))
    return jax.shard_map(body, mesh=mesh, in_specs=in_specs, out_specs=out_specs, check_vma=False)
```

```python
import functools

import jax
import jax.numpy as jnp
from jax import lax
from jax.experimental import pallas as pl
from jax.experimental.pallas import tpu as pltpu
from jax.sharding import PartitionSpec as P

NGROUP = 12
TILE = 512
TILE_OWN = 8
CAP = 2
ROWS = 8
HIGHEST = lax.Precision.HIGHEST
MESH = pl.DeviceIdType.MESH
F32 = jnp.float32
BF16 = jnp.bfloat16


def dot_nn(a, b):
    return lax.dot_general(a, b, (((1,), (0,)), ((), ())), precision=HIGHEST, preferred_element_type=F32)


def dot_nt(a, b):
    return lax.dot_general(a, b, (((1,), (1,)), ((), ())), precision=HIGHEST, preferred_element_type=F32)


def dot_tn(a, b):
    return lax.dot_general(a, b, (((0,), (0,)), ((), ())), precision=HIGHEST, preferred_element_type=F32)


def iota(shape, dim):
    return lax.broadcasted_iota(jnp.int32, shape, dim)


def dot_selected(selector, values):
    high = values.astype(BF16)
    rest = values - high.astype(F32)
    middle = rest.astype(BF16)
    low = (rest - middle.astype(F32)).astype(BF16)
    out = [jnp.dot(selector, part, preferred_element_type=F32) for part in (low, middle, high)]
    return (out[0] + out[1]) + out[2]


def to_column(row):
    size = row.shape[1]
    eye = iota((size, size), 0) == iota((size, size), 1)
    return jnp.sum(jnp.where(eye, row.astype(F32), 0.0), axis=1, keepdims=True)


def log2(value):
    assert value & (value - 1) == 0
    return value.bit_length() - 1


def inverse_spd(gram):
    size = gram.shape[0]
    wide = 2 * size
    eye = (iota((size, size), 0) == iota((size, size), 1)).astype(F32)
    joined = jnp.concatenate([eye, gram], axis=1)
    blocks = [joined[ROWS * b : ROWS * (b + 1), :] for b in range(size // ROWS)]
    row_of = iota((ROWS, wide), 0)
    for p in range(size // ROWS):
        spread = [
            [
                jnp.broadcast_to(block[:, size + p * ROWS + c : size + p * ROWS + c + 1], (ROWS, wide))
                for c in range(ROWS)
            ]
            for block in blocks
        ]
        panel = blocks[p]
        columns = list(spread[p])
        for k in range(ROWS):
            pivot = columns[k]
            scale = 1.0 / pivot[k : k + 1, :]
            here = row_of == k
            top = panel[k : k + 1, :] * scale
            panel = jnp.where(here, top, panel - pivot * top)
            for c in range(k + 1, ROWS):
                top = columns[c][k : k + 1, :] * scale
                columns[c] = jnp.where(here, top, columns[c] - pivot * top)
        for b in range(len(blocks)):
            if b == p:
                blocks[b] = panel
            else:
                terms = [spread[b][c] * panel[c : c + 1, :] for c in range(ROWS)]
                while len(terms) > 1:
                    terms = [x + y for x, y in zip(terms[::2], terms[1::2])]
                blocks[b] = blocks[b] - terms[0]
    return jnp.concatenate(blocks, axis=0)[:, :size]


def slot_codes(listed):
    owner = lax.shift_right_logical(listed, jnp.full(listed.shape, log2(TILE_OWN), jnp.int32)).astype(F32)
    lane = iota(listed.shape, 1)
    rank = jnp.zeros(listed.shape, F32)
    for j in range(listed.shape[1] - 1):
        rank += jnp.where((owner[:, j : j + 1] == owner) & (lane > j), 1.0, 0.0)
    return owner * CAP + rank


def kernel(
    wafers, spans,
    ts_ref, tm_hbm, bg_hbm, dw_hbm, cs_hbm, cl_hbm, pt_hbm, ht_hbm,
    fit_hbm, rx,
    tm_ref, bg_ref, dw_ref, cs_ref, cl_ref, pt_ref, ht_ref,
    ts_rx, ts_all, gr_rx, pj_rx, sw_ref, val_ref, hot_ref, left_ref, tx, fit_ref,
    span_send, span_recv, tile_send, tile_recv, local_sem,
):
    det_dev = ts_ref.shape[0]
    nt, span_len = tm_ref.shape
    det_w = pt_ref.shape[0]
    hits = ht_ref.shape[1]
    total = wafers * spans
    pix = TILE // wafers
    my_w, my_s = lax.axis_index("wafer"), lax.axis_index("span")
    me = my_w * spans + my_s

    s_peers = [lax.rem(my_s + i, spans) for i in range(spans)]
    w_peers = [lax.rem(my_w + i, wafers) for i in range(wafers)]
    others = s_peers[1:]

    def for_peers(act):
        if total <= 64:
            for s in range(spans):
                for w in range(wafers):
                    if w or s:
                        act(w_peers[w], s_peers[s])
        else:

            def step(i, carry):
                other = lax.rem(me + i, total)
                act(lax.div(other, spans), lax.rem(other, spans))
                return carry

            lax.fori_loop(1, total, step, 0)

    def own_start(s):
        return pl.multiple_of(s * span_len, span_len)

    pairs = (
        (tm_hbm, tm_ref),
        (ts_ref.at[:, pl.ds(own_start(my_s), span_len)], ts_rx.at[my_s]),
        (pt_hbm, pt_ref), (cs_hbm, cs_ref), (cl_hbm, cl_ref), (dw_hbm, dw_ref), (ht_hbm, ht_ref), (bg_hbm, bg_ref),
    )
    local = [pltpu.make_async_copy(a, b, local_sem.at[i]) for i, (a, b) in enumerate(pairs)]
    barrier = pltpu.get_barrier_semaphore()
    for_peers(
        lambda w, s: pl.semaphore_signal(barrier, inc=1, device_id=(w, s), device_id_type=MESH)
    )
    for copy in local:
        copy.start()
    pl.semaphore_wait(barrier, total - 1)

    def to_span(src, dst, which, s):
        pltpu.make_async_remote_copy(
            src_ref=src, dst_ref=dst, send_sem=span_send.at[which], recv_sem=span_recv.at[which],
            device_id=(my_w, s), device_id_type=MESH,
        ).start()

    def span_wait(buffer, sems, which):
        slots = buffer.at[pl.ds(0, spans - 1)]
        pltpu.make_async_copy(slots, slots, sems.at[which]).wait()

    for s in others:
        to_span(ts_ref.at[:, pl.ds(own_start(s), span_len)], ts_rx.at[my_s], 0, s)
    local[0].wait()
    templates = tm_ref[...]
    gr_rx[my_s] = dot_nt(templates, templates)
    for s in others:
        to_span(gr_rx.at[my_s], gr_rx.at[my_s], 1, s)

    for copy in local[2:]:
        copy.wait()

    code = slot_codes(ht_ref[...])
    own_code = jnp.sum(jnp.where(iota(code.shape, 0) == my_s, code, 0.0), axis=0, keepdims=True)
    slots = spans * CAP
    selector = (own_code == iota((slots, hits), 0).astype(F32)).astype(BF16)

    time = (iota((det_w, span_len), 1) + my_s * span_len).astype(F32)
    cut_start = to_column(cs_ref[...])
    cut_end = cut_start + to_column(cl_ref[...])
    inside = (time >= cut_start) & (time < cut_end)
    sw_ref[...] = jnp.where(inside, 0.0, to_column(dw_ref[...])).astype(BF16).astype(F32)

    coarse_count = wafers * hits
    coarse_iota = iota((coarse_count, span_len), 0)
    fine_iota = iota((pix, span_len), 0)

    def shifted(x, amount):
        return lax.shift_right_logical(x, jnp.full(x.shape, amount, jnp.int32))

    def coarse_of(points):
        return (shifted(points, log2(pix)) & (wafers - 1)) * hits + shifted(points, log2(TILE))

    groups = det_w // ROWS
    keep_left = left_ref.shape[0] == groups

    def place(coarse, values):
        return jnp.concatenate(
            [
                jnp.where(coarse_iota == coarse[r : r + 1, :], values[r : r + 1, :], 0.0).astype(BF16)
                for r in range(ROWS)
            ],
            axis=1,
        )

    def rows_of(g):
        return pl.ds(g * ROWS if isinstance(g, int) else pl.multiple_of(g * ROWS, ROWS), ROWS)

    def prepare(g, carry):
        points = pt_ref[rows_of(g), :]
        fine = points & (pix - 1)
        hot_ref[g] = jnp.concatenate(
            [jnp.where(fine_iota == fine[r : r + 1, :], 1.0, 0.0).astype(BF16) for r in range(ROWS)],
            axis=1,
        )
        if keep_left:
            left_ref[g] = place(coarse_of(points), sw_ref[rows_of(g), :])
        return carry

    lax.fori_loop(0, groups, prepare, 0, unroll=2)

    same_line = (bg_ref[...].astype(F32) == to_column(bg_ref[...])).astype(F32)
    local[1].wait()
    span_wait(ts_rx, span_recv, 0)
    for s in range(spans):
        ts_all[s * det_dev : (s + 1) * det_dev, :] = ts_rx[s]
    stream = ts_all[...]
    cleaned = stream - dot_nn(same_line, stream) * (NGROUP / det_w)
    pj_rx[my_s] = dot_nt(cleaned, templates)
    for s in others:
        to_span(pj_rx.at[my_s], pj_rx.at[my_s], 2, s)

    span_wait(gr_rx, span_recv, 1)
    inverse = inverse_spd(jnp.sum(gr_rx[...], axis=0))
    solved = dot_nn(inverse, templates)

    span_wait(pj_rx, span_recv, 2)
    projection = jnp.sum(pj_rx[...], axis=0)
    filtered = cleaned - dot_nn(projection, solved)
    val_ref[...] = (sw_ref[...] * filtered).astype(BF16).astype(F32)

    def bin_group(g, part):
        coarse = coarse_of(pt_ref[rows_of(g), :])
        weights = left_ref[g] if keep_left else place(coarse, sw_ref[rows_of(g), :])
        left = jnp.concatenate([place(coarse, val_ref[rows_of(g), :]), weights], axis=0)
        return part + lax.dot_general(
            left, hot_ref[g], (((1,), (1,)), ((), ())), preferred_element_type=F32
        )

    part = jnp.zeros((2 * coarse_count, pix), F32)
    if groups <= 8:
        for g in range(groups):
            part = bin_group(g, part)
    else:
        part = lax.fori_loop(0, groups, bin_group, part)

    wide = jnp.concatenate([part[q * hits : (q + 1) * hits, :] for q in range(2 * wafers)], axis=1)
    out = dot_selected(selector, wide)
    for q in range(wafers):
        for o in range(spans):
            for m in range(2):
                start = (m * wafers + q) * pix
                tx[q * spans + o, m * CAP : (m + 1) * CAP] = out[
                    o * CAP : (o + 1) * CAP, start : start + pix
                ]

    def send(w, s):
        pltpu.make_async_remote_copy(
            src_ref=tx.at[w * spans + s], dst_ref=rx.at[me],
            send_sem=tile_send, recv_sem=tile_recv,
            device_id=(w, s), device_id_type=MESH,
        ).start()

    for_peers(send)
    own = pltpu.make_async_copy(tx.at[me], rx.at[me], local_sem.at[0])
    own.start()

    mine = (iota((det_dev, det_w), 1) == iota((det_dev, det_w), 0) + my_s * det_dev).astype(F32)
    fit_ref[...] = dot_nn(dot_nn(mine, projection), inverse)
    fit = pltpu.make_async_copy(fit_ref, fit_hbm, local_sem.at[1])
    fit.start()
    for which, buffer in enumerate((ts_rx, gr_rx, pj_rx)):
        span_wait(buffer, span_send, which)
    own.wait()
    fit.wait()
    arrivals, departures = rx.at[pl.ds(0, total - 1)], tx.at[pl.ds(0, total - 1)]
    pltpu.make_async_copy(departures, departures, tile_send).wait()
    pltpu.make_async_copy(arrivals, arrivals, tile_recv).wait()


def collect(
    wafers, spans, rx_hbm, fit_hbm, ht_hbm, fit_out, rhs_ref, wgt_ref, rx, ht_ref, sems
):
    arrivals = pltpu.make_async_copy(rx_hbm, rx, sems.at[0])
    listing = pltpu.make_async_copy(ht_hbm, ht_ref, sems.at[1])
    fit = pltpu.make_async_copy(fit_hbm, fit_out, sems.at[2])
    listing.start()
    arrivals.start()
    fit.start()
    my_s = lax.axis_index("span")
    pix = rhs_ref.shape[1]
    listing.wait()
    listed = ht_ref[...]
    code = slot_codes(listed)
    place = (listed - (my_s * TILE_OWN - 1)).astype(F32)
    landing = [
        jnp.sum(jnp.where(code == (my_s * CAP + k).astype(F32), place, 0.0), axis=1, keepdims=True) - 1.0
        for k in range(CAP)
    ]
    row_iota = iota((TILE_OWN, pix), 0).astype(F32)
    sums = [jnp.zeros((TILE_OWN, pix), F32) for m in range(2)]
    arrivals.wait()
    for s in range(spans):
        arrived = rx[s]
        for w in range(1, wafers):
            arrived = arrived + rx[w * spans + s]
        for k in range(CAP):
            here = row_iota == landing[k][s : s + 1, :]
            for m in range(2):
                row = m * CAP + k
                sums[m] = sums[m] + jnp.where(here, arrived[row : row + 1, :], 0.0)
    rhs_ref[...] = sums[0]
    wgt_ref[...] = sums[1]
    fit.wait()


def body(timestream, templates, bias_group, det_weight, cut_start, cut_len, pointing, hit_tiles):
    wafers, spans = lax.axis_size("wafer"), lax.axis_size("span")
    det_dev = timestream.shape[0]
    nt, span_len = templates.shape
    det_w = pointing.shape[0]
    pix = TILE // wafers
    total = wafers * spans
    vmem = pl.BlockSpec(memory_space=pltpu.VMEM)
    anywhere = pl.BlockSpec(memory_space=pl.ANY)
    fit_shape = jax.ShapeDtypeStruct((det_dev, nt), F32)
    map_shape = jax.ShapeDtypeStruct((TILE_OWN, pix), F32)
    hits = hit_tiles.shape[1]
    groups = det_w // ROWS
    fit, tiles = pl.pallas_call(
        functools.partial(kernel, wafers, spans),
        out_shape=(fit_shape, jax.ShapeDtypeStruct((total, 2 * CAP, pix), F32)),
        in_specs=[anywhere] * 8,
        out_specs=(anywhere,) * 2,
        scratch_shapes=[
            pltpu.VMEM((nt, span_len), F32),
            pltpu.VMEM((1, det_w), jnp.int32),
            pltpu.VMEM((1, det_w), F32),
            pltpu.VMEM((1, det_w), jnp.int32),
            pltpu.VMEM((1, det_w), jnp.int32),
            pltpu.VMEM((det_w, span_len), jnp.int32),
            pltpu.VMEM(hit_tiles.shape, jnp.int32),
            pltpu.VMEM((spans, det_dev, span_len), F32),
            pltpu.VMEM((det_w, span_len), F32),
            pltpu.VMEM((spans, nt, nt), F32),
            pltpu.VMEM((spans, det_w, nt), F32),
            pltpu.VMEM((det_w, span_len), F32),
            pltpu.VMEM((det_w, span_len), F32),
            pltpu.VMEM((groups, pix, ROWS * span_len), BF16),
            pltpu.VMEM((groups if groups <= 8 else 1, wafers * hits, ROWS * span_len), BF16),
            pltpu.VMEM((total, 2 * CAP, pix), F32),
            pltpu.VMEM((det_dev, nt), F32),
            pltpu.SemaphoreType.DMA((3,)),
            pltpu.SemaphoreType.DMA((3,)),
            pltpu.SemaphoreType.DMA,
            pltpu.SemaphoreType.DMA,
            pltpu.SemaphoreType.DMA((8,)),
        ],
        compiler_params=pltpu.CompilerParams(
            collective_id=0, has_side_effects=True, vmem_limit_bytes=56 * 1024 * 1024
        ),
    )(
        timestream, templates, bias_group.reshape(1, det_w), det_weight.reshape(1, det_w),
        cut_start.reshape(1, det_w), cut_len.reshape(1, det_w), pointing, hit_tiles,
    )
    return pl.pallas_call(
        functools.partial(collect, wafers, spans),
        out_shape=(fit_shape, map_shape, map_shape),
        in_specs=[anywhere] * 3,
        out_specs=(anywhere, vmem, vmem),
        scratch_shapes=[
            pltpu.VMEM((total, 2 * CAP, pix), F32),
            pltpu.VMEM(hit_tiles.shape, jnp.int32),
            pltpu.SemaphoreType.DMA((3,)),
        ],
    )(tiles, fit, hit_tiles)


def solution(mesh):
    in_specs = (
        P(("wafer", "span"), None),
        P(None, "span"),
        P("wafer"),
        P("wafer"),
        P("wafer"),
        P("wafer"),
        P("wafer", "span"),
        P(),
    )
    out_specs = (P(("wafer", "span"), None), P("span", "wafer"), P("span", "wafer"))
    return jax.shard_map(body, mesh=mesh, in_specs=in_specs, out_specs=out_specs, check_vma=False)
```

```python
import functools

import jax
import jax.numpy as jnp
from jax import lax
from jax.experimental import pallas as pl
from jax.experimental.pallas import tpu as pltpu
from jax.sharding import PartitionSpec as P

NGROUP = 12
TILE = 512
TILE_OWN = 8
CAP = 2
ROWS = 8
HIGHEST = lax.Precision.HIGHEST
MESH = pl.DeviceIdType.MESH
F32 = jnp.float32
BF16 = jnp.bfloat16


def dot_nn(a, b):
    return lax.dot_general(a, b, (((1,), (0,)), ((), ())), precision=HIGHEST, preferred_element_type=F32)


def dot_nt(a, b):
    return lax.dot_general(a, b, (((1,), (1,)), ((), ())), precision=HIGHEST, preferred_element_type=F32)


def dot_tn(a, b):
    return lax.dot_general(a, b, (((0,), (0,)), ((), ())), precision=HIGHEST, preferred_element_type=F32)


def iota(shape, dim):
    return lax.broadcasted_iota(jnp.int32, shape, dim)


def dot_selected(selector, values):
    high = values.astype(BF16)
    rest = values - high.astype(F32)
    middle = rest.astype(BF16)
    low = (rest - middle.astype(F32)).astype(BF16)
    out = [jnp.dot(selector, part, preferred_element_type=F32) for part in (low, middle, high)]
    return (out[0] + out[1]) + out[2]


def to_column(row):
    size = row.shape[1]
    eye = iota((size, size), 0) == iota((size, size), 1)
    return jnp.sum(jnp.where(eye, row.astype(F32), 0.0), axis=1, keepdims=True)


def log2(value):
    assert value & (value - 1) == 0
    return value.bit_length() - 1


def inverse_spd(gram):
    size = gram.shape[0]
    wide = 2 * size
    eye = (iota((size, size), 0) == iota((size, size), 1)).astype(F32)
    joined = jnp.concatenate([eye, gram], axis=1)
    blocks = [joined[ROWS * b : ROWS * (b + 1), :] for b in range(size // ROWS)]
    row_of = iota((ROWS, wide), 0)
    for p in range(size // ROWS):
        spread = [
            [
                jnp.broadcast_to(block[:, size + p * ROWS + c : size + p * ROWS + c + 1], (ROWS, wide))
                for c in range(ROWS)
            ]
            for block in blocks
        ]
        panel = blocks[p]
        columns = list(spread[p])
        for k in range(ROWS):
            pivot = columns[k]
            scale = 1.0 / pivot[k : k + 1, :]
            here = row_of == k
            top = panel[k : k + 1, :] * scale
            panel = jnp.where(here, top, panel - pivot * top)
            for c in range(k + 1, ROWS):
                top = columns[c][k : k + 1, :] * scale
                columns[c] = jnp.where(here, top, columns[c] - pivot * top)
        for b in range(len(blocks)):
            if b == p:
                blocks[b] = panel
            else:
                terms = [spread[b][c] * panel[c : c + 1, :] for c in range(ROWS)]
                while len(terms) > 1:
                    terms = [x + y for x, y in zip(terms[::2], terms[1::2])]
                blocks[b] = blocks[b] - terms[0]
    return jnp.concatenate(blocks, axis=0)[:, :size]


def pack(tall):
    half = tall.shape[0] // 2
    return jnp.concatenate([tall[:half, :], tall[half:, :]], axis=1)


def unpack(wide):
    half = wide.shape[1] // 2
    return jnp.concatenate([wide[:, :half], wide[:, half:]], axis=0)


def slot_codes(listed):
    owner = lax.shift_right_logical(listed, jnp.full(listed.shape, log2(TILE_OWN), jnp.int32)).astype(F32)
    lane = iota(listed.shape, 1)
    rank = jnp.zeros(listed.shape, F32)
    for j in range(listed.shape[1] - 1):
        rank += jnp.where((owner[:, j : j + 1] == owner) & (lane > j), 1.0, 0.0)
    return owner * CAP + rank


def kernel(
    wafers, spans,
    ts_ref, tm_hbm, bg_hbm, dw_hbm, cs_hbm, cl_hbm, pt_hbm, ht_hbm,
    fit_hbm, rx,
    tm_ref, bg_ref, dw_ref, cs_ref, cl_ref, pt_ref, ht_ref,
    ts_rx, ts_all, gr_rx, pj_rx, sw_ref, val_ref, hot_ref, left_ref, wafer_tx, wafer_rx, tx, fit_ref,
    span_send, span_recv, wafer_send, wafer_recv, local_sem,
):
    det_dev = ts_ref.shape[0]
    nt, span_len = tm_ref.shape
    det_w = pt_ref.shape[0]
    hits = ht_ref.shape[1]
    pix = TILE // wafers
    my_w, my_s = lax.axis_index("wafer"), lax.axis_index("span")

    others = [lax.rem(my_s + i, spans) for i in range(1, spans)]
    other_wafers = [lax.rem(my_w + i, wafers) for i in range(1, wafers)]

    def own_start(s):
        return pl.multiple_of(s * span_len, span_len)

    pairs = (
        (tm_hbm, tm_ref),
        (ts_ref.at[:, pl.ds(own_start(my_s), span_len)], ts_rx.at[my_s]),
        (pt_hbm, pt_ref), (cs_hbm, cs_ref), (cl_hbm, cl_ref), (dw_hbm, dw_ref), (ht_hbm, ht_ref), (bg_hbm, bg_ref),
    )
    local = [pltpu.make_async_copy(a, b, local_sem.at[i]) for i, (a, b) in enumerate(pairs)]
    barrier = pltpu.get_barrier_semaphore()
    for s in others:
        pl.semaphore_signal(barrier, inc=1, device_id=(my_w, s), device_id_type=MESH)
    for w in other_wafers:
        pl.semaphore_signal(barrier, inc=1, device_id=(w, my_s), device_id_type=MESH)
    for copy in local:
        copy.start()
    pl.semaphore_wait(barrier, spans + wafers - 2)

    def to_span(src, dst, which, s):
        pltpu.make_async_remote_copy(
            src_ref=src, dst_ref=dst, send_sem=span_send.at[which], recv_sem=span_recv.at[which],
            device_id=(my_w, s), device_id_type=MESH,
        ).start()

    def span_wait(buffer, sems, which):
        slots = buffer.at[pl.ds(0, spans - 1)]
        pltpu.make_async_copy(slots, slots, sems.at[which]).wait()

    for s in others:
        to_span(ts_ref.at[:, pl.ds(own_start(s), span_len)], ts_rx.at[my_s], 0, s)
    local[0].wait()
    templates = tm_ref[...]
    gr_rx[my_s] = pack(dot_nt(templates, templates))
    for s in others:
        to_span(gr_rx.at[my_s], gr_rx.at[my_s], 1, s)

    for copy in local[2:]:
        copy.wait()

    code = slot_codes(ht_ref[...])
    own_code = jnp.sum(jnp.where(iota(code.shape, 0) == my_s, code, 0.0), axis=0, keepdims=True)
    slots = spans * CAP
    selector = (own_code == iota((slots, hits), 0).astype(F32)).astype(BF16)

    time = (iota((det_w, span_len), 1) + my_s * span_len).astype(F32)
    cut_start = to_column(cs_ref[...])
    cut_end = cut_start + to_column(cl_ref[...])
    inside = (time >= cut_start) & (time < cut_end)
    sw_ref[...] = jnp.where(inside, 0.0, to_column(dw_ref[...])).astype(BF16).astype(F32)

    coarse_count = wafers * hits
    coarse_iota = iota((coarse_count, span_len), 0)
    fine_iota = iota((pix, span_len), 0)

    def shifted(x, amount):
        return lax.shift_right_logical(x, jnp.full(x.shape, amount, jnp.int32))

    def coarse_of(points):
        return (shifted(points, log2(pix)) & (wafers - 1)) * hits + shifted(points, log2(TILE))

    groups = det_w // ROWS
    keep_left = left_ref.shape[0] == groups

    def place(coarse, values):
        return jnp.concatenate(
            [
                jnp.where(coarse_iota == coarse[r : r + 1, :], values[r : r + 1, :], 0.0).astype(BF16)
                for r in range(ROWS)
            ],
            axis=1,
        )

    def rows_of(g):
        return pl.ds(g * ROWS if isinstance(g, int) else pl.multiple_of(g * ROWS, ROWS), ROWS)

    def prepare(g, carry):
        points = pt_ref[rows_of(g), :]
        fine = points & (pix - 1)
        hot_ref[g] = jnp.concatenate(
            [jnp.where(fine_iota == fine[r : r + 1, :], 1.0, 0.0).astype(BF16) for r in range(ROWS)],
            axis=1,
        )
        if keep_left:
            left_ref[g] = place(coarse_of(points), sw_ref[rows_of(g), :])
        return carry

    lax.fori_loop(0, groups, prepare, 0, unroll=2)

    same_line = (bg_ref[...].astype(F32) == to_column(bg_ref[...])).astype(F32)
    local[1].wait()
    span_wait(ts_rx, span_recv, 0)
    for s in range(spans):
        ts_all[s * det_dev : (s + 1) * det_dev, :] = ts_rx[s]
    stream = ts_all[...]
    cleaned = stream - dot_nn(same_line, stream) * (NGROUP / det_w)
    pj_rx[my_s] = pack(dot_nt(cleaned, templates))
    for s in others:
        to_span(pj_rx.at[my_s], pj_rx.at[my_s], 2, s)

    span_wait(gr_rx, span_recv, 1)
    inverse = inverse_spd(unpack(jnp.sum(gr_rx[...], axis=0)))
    solved = dot_nn(inverse, templates)

    span_wait(pj_rx, span_recv, 2)
    projection = unpack(jnp.sum(pj_rx[...], axis=0))
    filtered = cleaned - dot_nn(projection, solved)
    val_ref[...] = (sw_ref[...] * filtered).astype(BF16).astype(F32)

    def bin_group(g, part):
        coarse = coarse_of(pt_ref[rows_of(g), :])
        weights = left_ref[g] if keep_left else place(coarse, sw_ref[rows_of(g), :])
        left = jnp.concatenate([place(coarse, val_ref[rows_of(g), :]), weights], axis=0)
        return part + lax.dot_general(
            left, hot_ref[g], (((1,), (1,)), ((), ())), preferred_element_type=F32
        )

    part = jnp.zeros((2 * coarse_count, pix), F32)
    if groups <= 8:
        for g in range(groups):
            part = bin_group(g, part)
    else:
        part = lax.fori_loop(0, groups, bin_group, part)

    for q in range(wafers):
        for m in range(2):
            start = (m * wafers + q) * hits
            wafer_tx[q, m * hits : (m + 1) * hits] = part[start : start + hits, :]
    for w in other_wafers:
        pltpu.make_async_remote_copy(
            src_ref=wafer_tx.at[w], dst_ref=wafer_rx.at[my_w],
            send_sem=wafer_send, recv_sem=wafer_recv,
            device_id=(w, my_s), device_id_type=MESH,
        ).start()
    wafer_rx[my_w] = wafer_tx[my_w]
    arrivals, departures = wafer_rx.at[pl.ds(0, wafers - 1)], wafer_tx.at[pl.ds(0, wafers - 1)]
    pltpu.make_async_copy(arrivals, arrivals, wafer_recv).wait()
    shared = jnp.sum(wafer_rx[...], axis=0)
    out = dot_selected(selector, jnp.concatenate([shared[:hits, :], shared[hits:, :]], axis=1))
    for o in range(spans):
        for m in range(2):
            tx[o, m * CAP : (m + 1) * CAP] = out[o * CAP : (o + 1) * CAP, m * pix : (m + 1) * pix]
    for s in others:
        to_span(tx.at[s], rx.at[my_s], 3, s)
    own = pltpu.make_async_copy(tx.at[my_s], rx.at[my_s], local_sem.at[0])
    own.start()

    mine = (iota((det_dev, det_w), 1) == iota((det_dev, det_w), 0) + my_s * det_dev).astype(F32)
    fit_ref[...] = dot_nn(dot_nn(mine, projection), inverse)
    fit = pltpu.make_async_copy(fit_ref, fit_hbm, local_sem.at[1])
    fit.start()
    for which, buffer in enumerate((ts_rx, gr_rx, pj_rx)):
        span_wait(buffer, span_send, which)
    own.wait()
    fit.wait()
    pltpu.make_async_copy(departures, departures, wafer_send).wait()
    span_wait(tx, span_send, 3)
    span_wait(rx, span_recv, 3)


def collect(
    rx_hbm, fit_hbm, ht_hbm, fit_out, rhs_ref, wgt_ref, rx, ht_ref, sems
):
    arrivals = pltpu.make_async_copy(rx_hbm, rx, sems.at[0])
    listing = pltpu.make_async_copy(ht_hbm, ht_ref, sems.at[1])
    fit = pltpu.make_async_copy(fit_hbm, fit_out, sems.at[2])
    listing.start()
    arrivals.start()
    fit.start()
    my_s = lax.axis_index("span")
    pix = rhs_ref.shape[1]
    listing.wait()
    listed = ht_ref[...]
    code = slot_codes(listed)
    place = (listed - (my_s * TILE_OWN - 1)).astype(F32)
    landing = [
        jnp.sum(jnp.where(code == (my_s * CAP + k).astype(F32), place, 0.0), axis=1, keepdims=True) - 1.0
        for k in range(CAP)
    ]
    row_iota = iota((TILE_OWN, pix), 0).astype(F32)
    sums = [jnp.zeros((TILE_OWN, pix), F32) for m in range(2)]
    arrivals.wait()
    for s in range(rx.shape[0]):
        arrived = rx[s]
        for k in range(CAP):
            here = row_iota == landing[k][s : s + 1, :]
            for m in range(2):
                row = m * CAP + k
                sums[m] = sums[m] + jnp.where(here, arrived[row : row + 1, :], 0.0)
    rhs_ref[...] = sums[0]
    wgt_ref[...] = sums[1]
    fit.wait()


def body(timestream, templates, bias_group, det_weight, cut_start, cut_len, pointing, hit_tiles):
    wafers, spans = lax.axis_size("wafer"), lax.axis_size("span")
    det_dev = timestream.shape[0]
    nt, span_len = templates.shape
    det_w = pointing.shape[0]
    pix = TILE // wafers
    vmem = pl.BlockSpec(memory_space=pltpu.VMEM)
    anywhere = pl.BlockSpec(memory_space=pl.ANY)
    fit_shape = jax.ShapeDtypeStruct((det_dev, nt), F32)
    map_shape = jax.ShapeDtypeStruct((TILE_OWN, pix), F32)
    hits = hit_tiles.shape[1]
    groups = det_w // ROWS
    fit, tiles = pl.pallas_call(
        functools.partial(kernel, wafers, spans),
        out_shape=(fit_shape, jax.ShapeDtypeStruct((spans, 2 * CAP, pix), F32)),
        in_specs=[anywhere] * 8,
        out_specs=(anywhere,) * 2,
        scratch_shapes=[
            pltpu.VMEM((nt, span_len), F32),
            pltpu.VMEM((1, det_w), jnp.int32),
            pltpu.VMEM((1, det_w), F32),
            pltpu.VMEM((1, det_w), jnp.int32),
            pltpu.VMEM((1, det_w), jnp.int32),
            pltpu.VMEM((det_w, span_len), jnp.int32),
            pltpu.VMEM(hit_tiles.shape, jnp.int32),
            pltpu.VMEM((spans, det_dev, span_len), F32),
            pltpu.VMEM((det_w, span_len), F32),
            pltpu.VMEM((spans, nt // 2, 2 * nt), F32),
            pltpu.VMEM((spans, det_w // 2, 2 * nt), F32),
            pltpu.VMEM((det_w, span_len), F32),
            pltpu.VMEM((det_w, span_len), F32),
            pltpu.VMEM((groups, pix, ROWS * span_len), BF16),
            pltpu.VMEM((groups if groups <= 8 else 1, wafers * hits, ROWS * span_len), BF16),
            pltpu.VMEM((wafers, 2 * hits, pix), F32),
            pltpu.VMEM((wafers, 2 * hits, pix), F32),
            pltpu.VMEM((spans, 2 * CAP, pix), F32),
            pltpu.VMEM((det_dev, nt), F32),
            pltpu.SemaphoreType.DMA((4,)),
            pltpu.SemaphoreType.DMA((4,)),
            pltpu.SemaphoreType.DMA,
            pltpu.SemaphoreType.DMA,
            pltpu.SemaphoreType.DMA((8,)),
        ],
        compiler_params=pltpu.CompilerParams(
            collective_id=0, has_side_effects=True, vmem_limit_bytes=56 * 1024 * 1024
        ),
    )(
        timestream, templates, bias_group.reshape(1, det_w), det_weight.reshape(1, det_w),
        cut_start.reshape(1, det_w), cut_len.reshape(1, det_w), pointing, hit_tiles,
    )
    return pl.pallas_call(
        collect,
        out_shape=(fit_shape, map_shape, map_shape),
        in_specs=[anywhere] * 3,
        out_specs=(anywhere, vmem, vmem),
        scratch_shapes=[
            pltpu.VMEM((spans, 2 * CAP, pix), F32),
            pltpu.VMEM(hit_tiles.shape, jnp.int32),
            pltpu.SemaphoreType.DMA((3,)),
        ],
    )(tiles, fit, hit_tiles)


def solution(mesh):
    in_specs = (
        P(("wafer", "span"), None),
        P(None, "span"),
        P("wafer"),
        P("wafer"),
        P("wafer"),
        P("wafer"),
        P("wafer", "span"),
        P(),
    )
    out_specs = (P(("wafer", "span"), None), P("span", "wafer"), P("span", "wafer"))
    return jax.shard_map(body, mesh=mesh, in_specs=in_specs, out_specs=out_specs, check_vma=False)
```

```python
import functools

import jax
import jax.numpy as jnp
from jax import lax
from jax.experimental import pallas as pl
from jax.experimental.pallas import tpu as pltpu
from jax.sharding import PartitionSpec as P

NGROUP = 12
TILE = 512
TILE_OWN = 8
CAP = 2
ROWS = 8
HIGHEST = lax.Precision.HIGHEST
MESH = pl.DeviceIdType.MESH
F32 = jnp.float32
BF16 = jnp.bfloat16


def dot_nn(a, b):
    return lax.dot_general(a, b, (((1,), (0,)), ((), ())), precision=HIGHEST, preferred_element_type=F32)


def dot_nt(a, b):
    return lax.dot_general(a, b, (((1,), (1,)), ((), ())), precision=HIGHEST, preferred_element_type=F32)


def dot_tn(a, b):
    return lax.dot_general(a, b, (((0,), (0,)), ((), ())), precision=HIGHEST, preferred_element_type=F32)


def iota(shape, dim):
    return lax.broadcasted_iota(jnp.int32, shape, dim)


def dot_selected(selector, values):
    high = values.astype(BF16)
    rest = values - high.astype(F32)
    middle = rest.astype(BF16)
    low = (rest - middle.astype(F32)).astype(BF16)
    out = [jnp.dot(selector, part, preferred_element_type=F32) for part in (low, middle, high)]
    return (out[0] + out[1]) + out[2]


def to_column(row):
    size = row.shape[1]
    eye = iota((size, size), 0) == iota((size, size), 1)
    return jnp.sum(jnp.where(eye, row.astype(F32), 0.0), axis=1, keepdims=True)


def log2(value):
    assert value & (value - 1) == 0
    return value.bit_length() - 1


def reciprocal(x):
    guess = pl.reciprocal(x, approx=True)
    guess = guess * (2.0 - x * guess)
    return guess * (2.0 - x * guess)


def inverse_spd(gram):
    size = gram.shape[0]
    wide = 2 * size
    eye = (iota((size, size), 0) == iota((size, size), 1)).astype(F32)
    joined = jnp.concatenate([eye, gram], axis=1)
    blocks = [joined[ROWS * b : ROWS * (b + 1), :] for b in range(size // ROWS)]
    row_of = iota((ROWS, wide), 0)
    for p in range(size // ROWS):
        spread = [
            [
                jnp.broadcast_to(block[:, size + p * ROWS + c : size + p * ROWS + c + 1], (ROWS, wide))
                for c in range(ROWS)
            ]
            for block in blocks
        ]
        panel = blocks[p]
        columns = list(spread[p])
        for k in range(ROWS):
            pivot = columns[k]
            here = row_of == k
            scale = reciprocal(jnp.broadcast_to(pivot[k : k + 1, :], (ROWS, wide)))

            def swept(block):
                top = block[k : k + 1, :]
                return jnp.where(here, 0.0, block) - jnp.where(here, -top, pivot * top) * scale

            panel = swept(panel)
            for c in range(k + 1, ROWS):
                columns[c] = swept(columns[c])
        for b in range(len(blocks)):
            if b == p:
                blocks[b] = panel
            else:
                terms = [spread[b][c] * panel[c : c + 1, :] for c in range(ROWS)]
                while len(terms) > 1:
                    terms = [x + y for x, y in zip(terms[::2], terms[1::2])]
                blocks[b] = blocks[b] - terms[0]
    return jnp.concatenate(blocks, axis=0)[:, :size]


def pack(tall):
    half = tall.shape[0] // 2
    return jnp.concatenate([tall[:half, :], tall[half:, :]], axis=1)


def unpack(wide):
    half = wide.shape[1] // 2
    return jnp.concatenate([wide[:, :half], wide[:, half:]], axis=0)


def slot_codes(listed):
    owner = lax.shift_right_logical(listed, jnp.full(listed.shape, log2(TILE_OWN), jnp.int32)).astype(F32)
    lane = iota(listed.shape, 1)
    rank = jnp.zeros(listed.shape, F32)
    for j in range(listed.shape[1] - 1):
        rank += jnp.where((owner[:, j : j + 1] == owner) & (lane > j), 1.0, 0.0)
    return owner * CAP + rank


def kernel(
    wafers, spans,
    ts_ref, tm_hbm, bg_hbm, dw_hbm, cs_hbm, cl_hbm, pt_hbm, ht_hbm,
    fit_hbm, rx, marks_hbm,
    tm_ref, bg_ref, dw_ref, cs_ref, cl_ref, pt_ref, ht_ref,
    ts_rx, ts_all, gr_rx, pj_rx, sw_ref, val_ref, hot_ref, left_ref, wafer_tx, wafer_rx, tx, fit_ref, marks_ref,
    span_send, span_recv, wafer_send, wafer_recv, local_sem,
):
    det_dev = ts_ref.shape[0]
    nt, span_len = tm_ref.shape
    det_w = pt_ref.shape[0]
    hits = ht_ref.shape[1]
    pix = TILE // wafers
    my_w, my_s = lax.axis_index("wafer"), lax.axis_index("span")

    others = [lax.rem(my_s + i, spans) for i in range(1, spans)]
    other_wafers = [lax.rem(my_w + i, wafers) for i in range(1, wafers)]

    def own_start(s):
        return pl.multiple_of(s * span_len, span_len)

    pairs = (
        (tm_hbm, tm_ref),
        (ts_ref.at[:, pl.ds(own_start(my_s), span_len)], ts_rx.at[my_s]),
        (pt_hbm, pt_ref), (cs_hbm, cs_ref), (cl_hbm, cl_ref), (dw_hbm, dw_ref), (ht_hbm, ht_ref), (bg_hbm, bg_ref),
    )
    local = [pltpu.make_async_copy(a, b, local_sem.at[i]) for i, (a, b) in enumerate(pairs)]
    barrier = pltpu.get_barrier_semaphore()
    for s in others:
        pl.semaphore_signal(barrier, inc=1, device_id=(my_w, s), device_id_type=MESH)
    for w in other_wafers:
        pl.semaphore_signal(barrier, inc=1, device_id=(w, my_s), device_id_type=MESH)
    for copy in local:
        copy.start()
    local[0].wait()
    templates = tm_ref[...]
    gr_rx[my_s] = pack(dot_nt(templates, templates))
    pl.semaphore_wait(barrier, spans + wafers - 2)

    def to_span(src, dst, which, s):
        pltpu.make_async_remote_copy(
            src_ref=src, dst_ref=dst, send_sem=span_send.at[which], recv_sem=span_recv.at[which],
            device_id=(my_w, s), device_id_type=MESH,
        ).start()

    def span_wait(buffer, sems, which):
        slots = buffer.at[pl.ds(0, spans - 1)]
        pltpu.make_async_copy(slots, slots, sems.at[which]).wait()

    for s in others:
        to_span(ts_ref.at[:, pl.ds(own_start(s), span_len)], ts_rx.at[my_s], 0, s)
    for s in others:
        to_span(gr_rx.at[my_s], gr_rx.at[my_s], 1, s)

    for copy in local[2:]:
        copy.wait()

    code = slot_codes(ht_ref[...])
    own_code = jnp.sum(jnp.where(iota(code.shape, 0) == my_s, code, 0.0), axis=0, keepdims=True)
    slots = spans * CAP
    selector = (own_code == iota((slots, hits), 0).astype(F32)).astype(BF16)

    place_of = (ht_ref[...] - (my_s * TILE_OWN - 1)).astype(F32)
    for k in range(CAP):
        mine = code == (my_s * CAP + k).astype(F32)
        landing = jnp.sum(jnp.where(mine, place_of, 0.0), axis=1, keepdims=True) - 1.0
        marks_ref[k] = jnp.broadcast_to(landing, (spans, pix))
    marks = pltpu.make_async_copy(marks_ref, marks_hbm, local_sem.at[2])
    marks.start()

    time = (iota((det_w, span_len), 1) + my_s * span_len).astype(F32)
    cut_start = to_column(cs_ref[...])
    cut_end = cut_start + to_column(cl_ref[...])
    inside = (time >= cut_start) & (time < cut_end)
    sw_ref[...] = jnp.where(inside, 0.0, to_column(dw_ref[...])).astype(BF16).astype(F32)

    coarse_count = wafers * hits
    coarse_iota = iota((coarse_count, span_len), 0)
    fine_iota = iota((pix, span_len), 0)

    def shifted(x, amount):
        return lax.shift_right_logical(x, jnp.full(x.shape, amount, jnp.int32))

    def coarse_of(points):
        return (shifted(points, log2(pix)) & (wafers - 1)) * hits + shifted(points, log2(TILE))

    groups = det_w // ROWS
    keep_left = left_ref.shape[0] == groups

    def place(coarse, values):
        return jnp.concatenate(
            [
                jnp.where(coarse_iota == coarse[r : r + 1, :], values[r : r + 1, :], 0.0).astype(BF16)
                for r in range(ROWS)
            ],
            axis=1,
        )

    def rows_of(g):
        return pl.ds(g * ROWS if isinstance(g, int) else pl.multiple_of(g * ROWS, ROWS), ROWS)

    def prepare(g, carry):
        points = pt_ref[rows_of(g), :]
        fine = points & (pix - 1)
        hot_ref[g] = jnp.concatenate(
            [jnp.where(fine_iota == fine[r : r + 1, :], 1.0, 0.0).astype(BF16) for r in range(ROWS)],
            axis=1,
        )
        if keep_left:
            left_ref[g] = place(coarse_of(points), sw_ref[rows_of(g), :])
        return carry

    lax.fori_loop(0, groups, prepare, 0, unroll=2)

    same_line = (bg_ref[...].astype(F32) == to_column(bg_ref[...])).astype(BF16)
    local[1].wait()
    span_wait(ts_rx, span_recv, 0)
    for s in range(spans):
        ts_all[s * det_dev : (s + 1) * det_dev, :] = ts_rx[s]
    stream = ts_all[...]
    cleaned = stream - dot_selected(same_line, stream) * (NGROUP / det_w)
    pj_rx[my_s] = pack(dot_nt(cleaned, templates))
    for s in others:
        to_span(pj_rx.at[my_s], pj_rx.at[my_s], 2, s)

    span_wait(gr_rx, span_recv, 1)
    inverse = inverse_spd(unpack(jnp.sum(gr_rx[...], axis=0)))
    solved = dot_nn(inverse, templates)

    span_wait(pj_rx, span_recv, 2)
    projection = unpack(jnp.sum(pj_rx[...], axis=0))
    filtered = cleaned - dot_nn(projection, solved)
    val_ref[...] = (sw_ref[...] * filtered).astype(BF16).astype(F32)

    def bin_group(g, part):
        coarse = coarse_of(pt_ref[rows_of(g), :])
        weights = left_ref[g] if keep_left else place(coarse, sw_ref[rows_of(g), :])
        left = jnp.concatenate([place(coarse, val_ref[rows_of(g), :]), weights], axis=0)
        return part + lax.dot_general(
            left, hot_ref[g], (((1,), (1,)), ((), ())), preferred_element_type=F32
        )

    part = jnp.zeros((2 * coarse_count, pix), F32)
    if groups <= 8:
        for g in range(groups):
            part = bin_group(g, part)
    else:
        part = lax.fori_loop(0, groups, bin_group, part)

    for q in range(wafers):
        for m in range(2):
            start = (m * wafers + q) * hits
            wafer_tx[q, m * hits : (m + 1) * hits] = part[start : start + hits, :]
    for w in other_wafers:
        pltpu.make_async_remote_copy(
            src_ref=wafer_tx.at[w], dst_ref=wafer_rx.at[my_w],
            send_sem=wafer_send, recv_sem=wafer_recv,
            device_id=(w, my_s), device_id_type=MESH,
        ).start()
    wafer_rx[my_w] = wafer_tx[my_w]
    arrivals, departures = wafer_rx.at[pl.ds(0, wafers - 1)], wafer_tx.at[pl.ds(0, wafers - 1)]
    pltpu.make_async_copy(arrivals, arrivals, wafer_recv).wait()
    shared = jnp.sum(wafer_rx[...], axis=0)
    out = dot_selected(selector, jnp.concatenate([shared[:hits, :], shared[hits:, :]], axis=1))
    for o in range(spans):
        for m in range(2):
            tx[o, m * CAP : (m + 1) * CAP] = out[o * CAP : (o + 1) * CAP, m * pix : (m + 1) * pix]
    for s in others:
        to_span(tx.at[s], rx.at[my_s], 3, s)
    own = pltpu.make_async_copy(tx.at[my_s], rx.at[my_s], local_sem.at[0])
    own.start()

    mine = (iota((det_dev, det_w), 1) == iota((det_dev, det_w), 0) + my_s * det_dev).astype(F32)
    fit_ref[...] = dot_nn(dot_nn(mine, projection), inverse)
    fit = pltpu.make_async_copy(fit_ref, fit_hbm, local_sem.at[1])
    fit.start()
    for which, buffer in enumerate((ts_rx, gr_rx, pj_rx)):
        span_wait(buffer, span_send, which)
    own.wait()
    fit.wait()
    marks.wait()
    pltpu.make_async_copy(departures, departures, wafer_send).wait()
    span_wait(tx, span_send, 3)
    span_wait(rx, span_recv, 3)


def collect(rx_hbm, fit_hbm, marks_hbm, fit_out, rhs_ref, wgt_ref, rx, marks_ref, sems):
    arrivals = pltpu.make_async_copy(rx_hbm, rx, sems.at[0])
    marks = pltpu.make_async_copy(marks_hbm, marks_ref, sems.at[1])
    fit = pltpu.make_async_copy(fit_hbm, fit_out, sems.at[2])
    marks.start()
    arrivals.start()
    fit.start()
    row_iota = iota(rhs_ref.shape, 0).astype(F32)
    sums = [jnp.zeros(rhs_ref.shape, F32) for m in range(2)]
    marks.wait()
    arrivals.wait()
    for s in range(rx.shape[0]):
        arrived = rx[s]
        for k in range(CAP):
            here = row_iota == marks_ref[k, s : s + 1, :]
            for m in range(2):
                row = m * CAP + k
                sums[m] = sums[m] + jnp.where(here, arrived[row : row + 1, :], 0.0)
    rhs_ref[...] = sums[0]
    wgt_ref[...] = sums[1]
    fit.wait()


def body(timestream, templates, bias_group, det_weight, cut_start, cut_len, pointing, hit_tiles):
    wafers, spans = lax.axis_size("wafer"), lax.axis_size("span")
    det_dev = timestream.shape[0]
    nt, span_len = templates.shape
    det_w = pointing.shape[0]
    pix = TILE // wafers
    vmem = pl.BlockSpec(memory_space=pltpu.VMEM)
    anywhere = pl.BlockSpec(memory_space=pl.ANY)
    fit_shape = jax.ShapeDtypeStruct((det_dev, nt), F32)
    map_shape = jax.ShapeDtypeStruct((TILE_OWN, pix), F32)
    hits = hit_tiles.shape[1]
    groups = det_w // ROWS
    marks_shape = (CAP, spans, pix)
    fit, tiles, marks = pl.pallas_call(
        functools.partial(kernel, wafers, spans),
        out_shape=(fit_shape, jax.ShapeDtypeStruct((spans, 2 * CAP, pix), F32), jax.ShapeDtypeStruct(marks_shape, F32)),
        in_specs=[anywhere] * 8,
        out_specs=(anywhere,) * 3,
        scratch_shapes=[
            pltpu.VMEM((nt, span_len), F32),
            pltpu.VMEM((1, det_w), jnp.int32),
            pltpu.VMEM((1, det_w), F32),
            pltpu.VMEM((1, det_w), jnp.int32),
            pltpu.VMEM((1, det_w), jnp.int32),
            pltpu.VMEM((det_w, span_len), jnp.int32),
            pltpu.VMEM(hit_tiles.shape, jnp.int32),
            pltpu.VMEM((spans, det_dev, span_len), F32),
            pltpu.VMEM((det_w, span_len), F32),
            pltpu.VMEM((spans, nt // 2, 2 * nt), F32),
            pltpu.VMEM((spans, det_w // 2, 2 * nt), F32),
            pltpu.VMEM((det_w, span_len), F32),
            pltpu.VMEM((det_w, span_len), F32),
            pltpu.VMEM((groups, pix, ROWS * span_len), BF16),
            pltpu.VMEM((groups if groups <= 8 else 1, wafers * hits, ROWS * span_len), BF16),
            pltpu.VMEM((wafers, 2 * hits, pix), F32),
            pltpu.VMEM((wafers, 2 * hits, pix), F32),
            pltpu.VMEM((spans, 2 * CAP, pix), F32),
            pltpu.VMEM((det_dev, nt), F32),
            pltpu.VMEM(marks_shape, F32),
            pltpu.SemaphoreType.DMA((4,)),
            pltpu.SemaphoreType.DMA((4,)),
            pltpu.SemaphoreType.DMA,
            pltpu.SemaphoreType.DMA,
            pltpu.SemaphoreType.DMA((8,)),
        ],
        compiler_params=pltpu.CompilerParams(
            collective_id=0, has_side_effects=True, vmem_limit_bytes=56 * 1024 * 1024
        ),
    )(
        timestream, templates, bias_group.reshape(1, det_w), det_weight.reshape(1, det_w),
        cut_start.reshape(1, det_w), cut_len.reshape(1, det_w), pointing, hit_tiles,
    )
    return pl.pallas_call(
        collect,
        out_shape=(fit_shape, map_shape, map_shape),
        in_specs=[anywhere] * 3,
        out_specs=(anywhere, vmem, vmem),
        scratch_shapes=[
            pltpu.VMEM((spans, 2 * CAP, pix), F32),
            pltpu.VMEM(marks_shape, F32),
            pltpu.SemaphoreType.DMA((3,)),
        ],
    )(tiles, fit, marks)


def solution(mesh):
    in_specs = (
        P(("wafer", "span"), None),
        P(None, "span"),
        P("wafer"),
        P("wafer"),
        P("wafer"),
        P("wafer"),
        P("wafer", "span"),
        P(),
    )
    out_specs = (P(("wafer", "span"), None), P("span", "wafer"), P("span", "wafer"))
    return jax.shard_map(body, mesh=mesh, in_specs=in_specs, out_specs=out_specs, check_vma=False)
```

```python
import functools

import jax
import jax.numpy as jnp
from jax import lax
from jax.experimental import pallas as pl
from jax.experimental.pallas import tpu as pltpu
from jax.sharding import PartitionSpec as P

NGROUP = 12
TILE = 512
TILE_OWN = 8
CAP = 2
ROWS = 8
HIGHEST = lax.Precision.HIGHEST
MESH = pl.DeviceIdType.MESH
F32 = jnp.float32
BF16 = jnp.bfloat16


def dot_nn(a, b):
    return lax.dot_general(a, b, (((1,), (0,)), ((), ())), precision=HIGHEST, preferred_element_type=F32)


def dot_nt(a, b):
    return lax.dot_general(a, b, (((1,), (1,)), ((), ())), precision=HIGHEST, preferred_element_type=F32)


def dot_tn(a, b):
    return lax.dot_general(a, b, (((0,), (0,)), ((), ())), precision=HIGHEST, preferred_element_type=F32)


def iota(shape, dim):
    return lax.broadcasted_iota(jnp.int32, shape, dim)


def dot_selected(selector, values):
    high = values.astype(BF16)
    rest = values - high.astype(F32)
    middle = rest.astype(BF16)
    low = (rest - middle.astype(F32)).astype(BF16)
    out = [jnp.dot(selector, part, preferred_element_type=F32) for part in (low, middle, high)]
    return (out[0] + out[1]) + out[2]


def to_column(row):
    size = row.shape[1]
    eye = iota((size, size), 0) == iota((size, size), 1)
    return jnp.sum(jnp.where(eye, row.astype(F32), 0.0), axis=1, keepdims=True)


def log2(value):
    assert value & (value - 1) == 0
    return value.bit_length() - 1


def reciprocal(x):
    guess = pl.reciprocal(x, approx=True)
    guess = guess * (2.0 - x * guess)
    return guess * (2.0 - x * guess)


def inverse_spd(twice):
    size, wide = twice.shape
    lane = iota(twice.shape, 1)
    eye = (iota(twice.shape, 0) == lane).astype(F32)
    joined = jnp.where(lane < size, eye, twice)
    blocks = [joined[ROWS * b : ROWS * (b + 1), :] for b in range(size // ROWS)]
    row_of = iota((ROWS, wide), 0)
    for p in range(size // ROWS):
        spread = [
            [
                jnp.broadcast_to(block[:, size + p * ROWS + c : size + p * ROWS + c + 1], (ROWS, wide))
                for c in range(ROWS)
            ]
            for block in blocks
        ]
        panel = blocks[p]
        columns = list(spread[p])
        for k in range(ROWS):
            pivot = columns[k]
            here = row_of == k
            scale = reciprocal(jnp.broadcast_to(pivot[k : k + 1, :], (ROWS, wide)))

            def swept(block):
                top = block[k : k + 1, :]
                return jnp.where(here, 0.0, block) - jnp.where(here, -top, pivot * top) * scale

            panel = swept(panel)
            for c in range(k + 1, ROWS):
                columns[c] = swept(columns[c])
        for b in range(len(blocks)):
            if b == p:
                blocks[b] = panel
            else:
                terms = [spread[b][c] * panel[c : c + 1, :] for c in range(ROWS)]
                while len(terms) > 1:
                    terms = [x + y for x, y in zip(terms[::2], terms[1::2])]
                blocks[b] = blocks[b] - terms[0]
    return jnp.concatenate(blocks, axis=0)[:, :size]


def pack(tall):
    half = tall.shape[0] // 2
    return jnp.concatenate([tall[:half, :], tall[half:, :]], axis=1)


def unpack(wide):
    half = wide.shape[1] // 2
    return jnp.concatenate([wide[:, :half], wide[:, half:]], axis=0)


def slot_codes(listed):
    owner = lax.shift_right_logical(listed, jnp.full(listed.shape, log2(TILE_OWN), jnp.int32)).astype(F32)
    lane = iota(listed.shape, 1)
    rank = jnp.zeros(listed.shape, F32)
    for j in range(listed.shape[1] - 1):
        rank += jnp.where((owner[:, j : j + 1] == owner) & (lane > j), 1.0, 0.0)
    return owner * CAP + rank


def kernel(
    wafers, spans,
    ts_ref, tm_hbm, bg_hbm, dw_hbm, cs_hbm, cl_hbm, pt_hbm, ht_hbm,
    fit_hbm, rx, marks_hbm,
    tm_ref, bg_ref, dw_ref, cs_ref, cl_ref, pt_ref, ht_ref,
    ts_rx, ts_all, gr_tx, gr_rx, gr_all, pj_rx, sw_ref, val_ref, hot_ref, left_ref, wafer_tx, wafer_rx, tx, fit_ref, marks_ref,
    span_send, span_recv, wafer_send, wafer_recv, local_sem,
):
    det_dev = ts_ref.shape[0]
    nt, span_len = tm_ref.shape
    det_w = pt_ref.shape[0]
    hits = ht_ref.shape[1]
    pix = TILE // wafers
    my_w, my_s = lax.axis_index("wafer"), lax.axis_index("span")

    others = [lax.rem(my_s + i, spans) for i in range(1, spans)]
    other_wafers = [lax.rem(my_w + i, wafers) for i in range(1, wafers)]

    def own_start(s):
        return pl.multiple_of(s * span_len, span_len)

    pairs = (
        (tm_hbm, tm_ref),
        (ts_ref.at[:, pl.ds(own_start(my_s), span_len)], ts_rx.at[my_s]),
        (pt_hbm, pt_ref), (cs_hbm, cs_ref), (cl_hbm, cl_ref), (dw_hbm, dw_ref), (ht_hbm, ht_ref), (bg_hbm, bg_ref),
    )
    local = [pltpu.make_async_copy(a, b, local_sem.at[i]) for i, (a, b) in enumerate(pairs)]
    barrier = pltpu.get_barrier_semaphore()
    for s in others:
        pl.semaphore_signal(barrier, inc=1, device_id=(my_w, s), device_id_type=MESH)
    for w in other_wafers:
        pl.semaphore_signal(barrier, inc=1, device_id=(w, my_s), device_id_type=MESH)
    for copy in local:
        copy.start()
    local[0].wait()
    templates = tm_ref[...]
    twice = dot_nt(templates, jnp.concatenate([templates, templates], axis=0))
    piece = nt // spans
    for s in range(spans):
        gr_tx[s] = twice[s * piece : (s + 1) * piece, :]
    gr_rx[my_s] = gr_tx[my_s]
    pl.semaphore_wait(barrier, spans + wafers - 2)

    def to_span(src, dst, which, s):
        pltpu.make_async_remote_copy(
            src_ref=src, dst_ref=dst, send_sem=span_send.at[which], recv_sem=span_recv.at[which],
            device_id=(my_w, s), device_id_type=MESH,
        ).start()

    def span_wait(buffer, sems, which):
        slots = buffer.at[pl.ds(0, spans - 1)]
        pltpu.make_async_copy(slots, slots, sems.at[which]).wait()

    for s in others:
        to_span(ts_ref.at[:, pl.ds(own_start(s), span_len)], ts_rx.at[my_s], 0, s)
    for s in others:
        to_span(gr_tx.at[s], gr_rx.at[my_s], 1, s)

    for copy in local[2:]:
        copy.wait()

    code = slot_codes(ht_ref[...])
    own_code = jnp.sum(jnp.where(iota(code.shape, 0) == my_s, code, 0.0), axis=0, keepdims=True)
    slots = spans * CAP
    selector = (own_code == iota((slots, hits), 0).astype(F32)).astype(BF16)

    place_of = (ht_ref[...] - (my_s * TILE_OWN - 1)).astype(F32)
    for k in range(CAP):
        mine = code == (my_s * CAP + k).astype(F32)
        landing = jnp.sum(jnp.where(mine, place_of, 0.0), axis=1, keepdims=True) - 1.0
        marks_ref[k] = jnp.broadcast_to(landing, (spans, pix))
    marks = pltpu.make_async_copy(marks_ref, marks_hbm, local_sem.at[2])
    marks.start()

    time = (iota((det_w, span_len), 1) + my_s * span_len).astype(F32)
    cut_start = to_column(cs_ref[...])
    cut_end = cut_start + to_column(cl_ref[...])
    inside = (time >= cut_start) & (time < cut_end)
    sw_ref[...] = jnp.where(inside, 0.0, to_column(dw_ref[...])).astype(BF16).astype(F32)

    coarse_count = wafers * hits
    coarse_iota = iota((coarse_count, span_len), 0)
    fine_iota = iota((pix, span_len), 0)

    def shifted(x, amount):
        return lax.shift_right_logical(x, jnp.full(x.shape, amount, jnp.int32))

    def coarse_of(points):
        return (shifted(points, log2(pix)) & (wafers - 1)) * hits + shifted(points, log2(TILE))

    groups = det_w // ROWS
    keep_left = left_ref.shape[0] == groups

    def place(coarse, values):
        return jnp.concatenate(
            [
                jnp.where(coarse_iota == coarse[r : r + 1, :], values[r : r + 1, :], 0.0).astype(BF16)
                for r in range(ROWS)
            ],
            axis=1,
        )

    def rows_of(g):
        return pl.ds(g * ROWS if isinstance(g, int) else pl.multiple_of(g * ROWS, ROWS), ROWS)

    def prepare(g, carry):
        points = pt_ref[rows_of(g), :]
        fine = points & (pix - 1)
        hot_ref[g] = jnp.concatenate(
            [jnp.where(fine_iota == fine[r : r + 1, :], 1.0, 0.0).astype(BF16) for r in range(ROWS)],
            axis=1,
        )
        if keep_left:
            left_ref[g] = place(coarse_of(points), sw_ref[rows_of(g), :])
        return carry

    lax.fori_loop(0, groups, prepare, 0, unroll=2)

    same_line = (bg_ref[...].astype(F32) == to_column(bg_ref[...])).astype(BF16)
    span_wait(gr_rx, span_recv, 1)
    gr_all[my_s] = jnp.sum(gr_rx[...], axis=0)
    for s in others:
        to_span(gr_all.at[my_s], gr_all.at[my_s], 4, s)
    local[1].wait()
    span_wait(ts_rx, span_recv, 0)
    for s in range(spans):
        ts_all[s * det_dev : (s + 1) * det_dev, :] = ts_rx[s]
    stream = ts_all[...]
    cleaned = stream - dot_selected(same_line, stream) * (NGROUP / det_w)
    pj_rx[my_s] = pack(dot_nt(cleaned, templates))
    for s in others:
        to_span(pj_rx.at[my_s], pj_rx.at[my_s], 2, s)

    span_wait(gr_all, span_recv, 4)
    inverse = inverse_spd(jnp.concatenate([gr_all[s] for s in range(spans)], axis=0))
    solved = dot_nn(inverse, templates)

    span_wait(pj_rx, span_recv, 2)
    projection = unpack(jnp.sum(pj_rx[...], axis=0))
    filtered = cleaned - dot_nn(projection, solved)
    val_ref[...] = (sw_ref[...] * filtered).astype(BF16).astype(F32)

    def bin_group(g, part):
        coarse = coarse_of(pt_ref[rows_of(g), :])
        weights = left_ref[g] if keep_left else place(coarse, sw_ref[rows_of(g), :])
        left = jnp.concatenate([place(coarse, val_ref[rows_of(g), :]), weights], axis=0)
        return part + lax.dot_general(
            left, hot_ref[g], (((1,), (1,)), ((), ())), preferred_element_type=F32
        )

    part = jnp.zeros((2 * coarse_count, pix), F32)
    if groups <= 8:
        for g in range(groups):
            part = bin_group(g, part)
    else:
        part = lax.fori_loop(0, groups, bin_group, part)

    for q in range(wafers):
        for m in range(2):
            start = (m * wafers + q) * hits
            wafer_tx[q, m * hits : (m + 1) * hits] = part[start : start + hits, :]
    for w in other_wafers:
        pltpu.make_async_remote_copy(
            src_ref=wafer_tx.at[w], dst_ref=wafer_rx.at[my_w],
            send_sem=wafer_send, recv_sem=wafer_recv,
            device_id=(w, my_s), device_id_type=MESH,
        ).start()
    wafer_rx[my_w] = wafer_tx[my_w]
    arrivals, departures = wafer_rx.at[pl.ds(0, wafers - 1)], wafer_tx.at[pl.ds(0, wafers - 1)]
    pltpu.make_async_copy(arrivals, arrivals, wafer_recv).wait()
    shared = jnp.sum(wafer_rx[...], axis=0)
    out = dot_selected(selector, jnp.concatenate([shared[:hits, :], shared[hits:, :]], axis=1))
    for o in range(spans):
        for m in range(2):
            tx[o, m * CAP : (m + 1) * CAP] = out[o * CAP : (o + 1) * CAP, m * pix : (m + 1) * pix]
    for s in others:
        to_span(tx.at[s], rx.at[my_s], 3, s)
    own = pltpu.make_async_copy(tx.at[my_s], rx.at[my_s], local_sem.at[0])
    own.start()

    mine = (iota((det_dev, det_w), 1) == iota((det_dev, det_w), 0) + my_s * det_dev).astype(F32)
    fit_ref[...] = dot_nn(dot_nn(mine, projection), inverse)
    fit = pltpu.make_async_copy(fit_ref, fit_hbm, local_sem.at[1])
    fit.start()
    for which, buffer in ((0, ts_rx), (1, gr_rx), (2, pj_rx), (4, gr_all)):
        span_wait(buffer, span_send, which)
    own.wait()
    fit.wait()
    marks.wait()
    pltpu.make_async_copy(departures, departures, wafer_send).wait()
    span_wait(tx, span_send, 3)
    span_wait(rx, span_recv, 3)


def collect(rx_hbm, fit_hbm, marks_hbm, fit_out, rhs_ref, wgt_ref, rx, marks_ref, sems):
    arrivals = pltpu.make_async_copy(rx_hbm, rx, sems.at[0])
    marks = pltpu.make_async_copy(marks_hbm, marks_ref, sems.at[1])
    fit = pltpu.make_async_copy(fit_hbm, fit_out, sems.at[2])
    marks.start()
    arrivals.start()
    fit.start()
    row_iota = iota(rhs_ref.shape, 0).astype(F32)
    sums = [jnp.zeros(rhs_ref.shape, F32) for m in range(2)]
    marks.wait()
    arrivals.wait()
    for s in range(rx.shape[0]):
        arrived = rx[s]
        for k in range(CAP):
            here = row_iota == marks_ref[k, s : s + 1, :]
            for m in range(2):
                row = m * CAP + k
                sums[m] = sums[m] + jnp.where(here, arrived[row : row + 1, :], 0.0)
    rhs_ref[...] = sums[0]
    wgt_ref[...] = sums[1]
    fit.wait()


def body(timestream, templates, bias_group, det_weight, cut_start, cut_len, pointing, hit_tiles):
    wafers, spans = lax.axis_size("wafer"), lax.axis_size("span")
    det_dev = timestream.shape[0]
    nt, span_len = templates.shape
    det_w = pointing.shape[0]
    pix = TILE // wafers
    vmem = pl.BlockSpec(memory_space=pltpu.VMEM)
    anywhere = pl.BlockSpec(memory_space=pl.ANY)
    fit_shape = jax.ShapeDtypeStruct((det_dev, nt), F32)
    map_shape = jax.ShapeDtypeStruct((TILE_OWN, pix), F32)
    hits = hit_tiles.shape[1]
    groups = det_w // ROWS
    marks_shape = (CAP, spans, pix)
    fit, tiles, marks = pl.pallas_call(
        functools.partial(kernel, wafers, spans),
        out_shape=(fit_shape, jax.ShapeDtypeStruct((spans, 2 * CAP, pix), F32), jax.ShapeDtypeStruct(marks_shape, F32)),
        in_specs=[anywhere] * 8,
        out_specs=(anywhere,) * 3,
        scratch_shapes=[
            pltpu.VMEM((nt, span_len), F32),
            pltpu.VMEM((1, det_w), jnp.int32),
            pltpu.VMEM((1, det_w), F32),
            pltpu.VMEM((1, det_w), jnp.int32),
            pltpu.VMEM((1, det_w), jnp.int32),
            pltpu.VMEM((det_w, span_len), jnp.int32),
            pltpu.VMEM(hit_tiles.shape, jnp.int32),
            pltpu.VMEM((spans, det_dev, span_len), F32),
            pltpu.VMEM((det_w, span_len), F32),
            pltpu.VMEM((spans, nt // spans, 2 * nt), F32),
            pltpu.VMEM((spans, nt // spans, 2 * nt), F32),
            pltpu.VMEM((spans, nt // spans, 2 * nt), F32),
            pltpu.VMEM((spans, det_w // 2, 2 * nt), F32),
            pltpu.VMEM((det_w, span_len), F32),
            pltpu.VMEM((det_w, span_len), F32),
            pltpu.VMEM((groups, pix, ROWS * span_len), BF16),
            pltpu.VMEM((groups if groups <= 8 else 1, wafers * hits, ROWS * span_len), BF16),
            pltpu.VMEM((wafers, 2 * hits, pix), F32),
            pltpu.VMEM((wafers, 2 * hits, pix), F32),
            pltpu.VMEM((spans, 2 * CAP, pix), F32),
            pltpu.VMEM((det_dev, nt), F32),
            pltpu.VMEM(marks_shape, F32),
            pltpu.SemaphoreType.DMA((5,)),
            pltpu.SemaphoreType.DMA((5,)),
            pltpu.SemaphoreType.DMA,
            pltpu.SemaphoreType.DMA,
            pltpu.SemaphoreType.DMA((8,)),
        ],
        compiler_params=pltpu.CompilerParams(
            collective_id=0, has_side_effects=True, vmem_limit_bytes=56 * 1024 * 1024
        ),
    )(
        timestream, templates, bias_group.reshape(1, det_w), det_weight.reshape(1, det_w),
        cut_start.reshape(1, det_w), cut_len.reshape(1, det_w), pointing, hit_tiles,
    )
    return pl.pallas_call(
        collect,
        out_shape=(fit_shape, map_shape, map_shape),
        in_specs=[anywhere] * 3,
        out_specs=(anywhere, vmem, vmem),
        scratch_shapes=[
            pltpu.VMEM((spans, 2 * CAP, pix), F32),
            pltpu.VMEM(marks_shape, F32),
            pltpu.SemaphoreType.DMA((3,)),
        ],
    )(tiles, fit, marks)


def solution(mesh):
    in_specs = (
        P(("wafer", "span"), None),
        P(None, "span"),
        P("wafer"),
        P("wafer"),
        P("wafer"),
        P("wafer"),
        P("wafer", "span"),
        P(),
    )
    out_specs = (P(("wafer", "span"), None), P("span", "wafer"), P("span", "wafer"))
    return jax.shard_map(body, mesh=mesh, in_specs=in_specs, out_specs=out_specs, check_vma=False)
```

```python
import functools

import jax
import jax.numpy as jnp
from jax import lax
from jax.experimental import pallas as pl
from jax.experimental.pallas import tpu as pltpu
from jax.sharding import PartitionSpec as P

NGROUP = 12
TILE = 512
TILE_OWN = 8
CAP = 2
ROWS = 8
HIGHEST = lax.Precision.HIGHEST
MESH = pl.DeviceIdType.MESH
F32 = jnp.float32
BF16 = jnp.bfloat16


def dot_nn(a, b):
    return lax.dot_general(a, b, (((1,), (0,)), ((), ())), precision=HIGHEST, preferred_element_type=F32)


def dot_nt(a, b):
    return lax.dot_general(a, b, (((1,), (1,)), ((), ())), precision=HIGHEST, preferred_element_type=F32)


def dot_tn(a, b):
    return lax.dot_general(a, b, (((0,), (0,)), ((), ())), precision=HIGHEST, preferred_element_type=F32)


def iota(shape, dim):
    return lax.broadcasted_iota(jnp.int32, shape, dim)


def dot_selected(selector, values):
    high = values.astype(BF16)
    rest = values - high.astype(F32)
    middle = rest.astype(BF16)
    low = (rest - middle.astype(F32)).astype(BF16)
    out = [jnp.dot(selector, part, preferred_element_type=F32) for part in (low, middle, high)]
    return (out[0] + out[1]) + out[2]


def to_column(row):
    size = row.shape[1]
    eye = iota((size, size), 0) == iota((size, size), 1)
    return jnp.sum(jnp.where(eye, row.astype(F32), 0.0), axis=1, keepdims=True)


def log2(value):
    assert value & (value - 1) == 0
    return value.bit_length() - 1


def inverse_spd(gram):
    size = gram.shape[0]
    wide = 2 * size
    eye = (iota((size, size), 0) == iota((size, size), 1)).astype(F32)
    joined = jnp.concatenate([eye, gram], axis=1)
    blocks = [joined[ROWS * b : ROWS * (b + 1), :] for b in range(size // ROWS)]
    row_of = iota((ROWS, wide), 0)
    for p in range(size // ROWS):
        spread = [
            [
                jnp.broadcast_to(block[:, size + p * ROWS + c : size + p * ROWS + c + 1], (ROWS, wide))
                for c in range(ROWS)
            ]
            for block in blocks
        ]
        panel = blocks[p]
        columns = list(spread[p])
        for k in range(ROWS):
            pivot = columns[k]
            scale = 1.0 / pivot[k : k + 1, :]
            here = row_of == k
            top = panel[k : k + 1, :] * scale
            panel = jnp.where(here, top, panel - pivot * top)
            for c in range(k + 1, ROWS):
                top = columns[c][k : k + 1, :] * scale
                columns[c] = jnp.where(here, top, columns[c] - pivot * top)
        for b in range(len(blocks)):
            if b == p:
                blocks[b] = panel
            else:
                terms = [spread[b][c] * panel[c : c + 1, :] for c in range(ROWS)]
                while len(terms) > 1:
                    terms = [x + y for x, y in zip(terms[::2], terms[1::2])]
                blocks[b] = blocks[b] - terms[0]
    return jnp.concatenate(blocks, axis=0)[:, :size]


def pack(tall):
    half = tall.shape[0] // 2
    return jnp.concatenate([tall[:half, :], tall[half:, :]], axis=1)


def unpack(wide):
    half = wide.shape[1] // 2
    return jnp.concatenate([wide[:, :half], wide[:, half:]], axis=0)


def slot_codes(listed):
    owner = lax.shift_right_logical(listed, jnp.full(listed.shape, log2(TILE_OWN), jnp.int32)).astype(F32)
    lane = iota(listed.shape, 1)
    rank = jnp.zeros(listed.shape, F32)
    for j in range(listed.shape[1] - 1):
        rank += jnp.where((owner[:, j : j + 1] == owner) & (lane > j), 1.0, 0.0)
    return owner * CAP + rank


def kernel(
    wafers, spans,
    ts_ref, tm_hbm, bg_hbm, dw_hbm, cs_hbm, cl_hbm, pt_hbm, ht_hbm,
    fit_hbm, rx,
    tm_ref, bg_ref, dw_ref, cs_ref, cl_ref, pt_ref, ht_ref,
    ts_rx, ts_all, gr_rx, pj_rx, sw_ref, val_ref, hot_ref, left_ref, wafer_tx, wafer_rx, tx, fit_ref,
    span_send, span_recv, wafer_send, wafer_recv, local_sem,
):
    det_dev = ts_ref.shape[0]
    nt, span_len = tm_ref.shape
    det_w = pt_ref.shape[0]
    hits = ht_ref.shape[1]
    pix = TILE // wafers
    my_w, my_s = lax.axis_index("wafer"), lax.axis_index("span")

    others = [lax.rem(my_s + i, spans) for i in range(1, spans)]
    other_wafers = [lax.rem(my_w + i, wafers) for i in range(1, wafers)]

    def own_start(s):
        return pl.multiple_of(s * span_len, span_len)

    pairs = (
        (tm_hbm, tm_ref),
        (ts_ref.at[:, pl.ds(own_start(my_s), span_len)], ts_rx.at[my_s]),
        (pt_hbm, pt_ref), (cs_hbm, cs_ref), (cl_hbm, cl_ref), (dw_hbm, dw_ref), (ht_hbm, ht_ref), (bg_hbm, bg_ref),
    )
    local = [pltpu.make_async_copy(a, b, local_sem.at[i]) for i, (a, b) in enumerate(pairs)]
    barrier = pltpu.get_barrier_semaphore()
    for s in others:
        pl.semaphore_signal(barrier, inc=1, device_id=(my_w, s), device_id_type=MESH)
    for w in other_wafers:
        pl.semaphore_signal(barrier, inc=1, device_id=(w, my_s), device_id_type=MESH)
    for copy in local:
        copy.start()
    pl.semaphore_wait(barrier, spans + wafers - 2)

    def to_span(src, dst, which, s):
        pltpu.make_async_remote_copy(
            src_ref=src, dst_ref=dst, send_sem=span_send.at[which], recv_sem=span_recv.at[which],
            device_id=(my_w, s), device_id_type=MESH,
        ).start()

    def span_wait(buffer, sems, which):
        slots = buffer.at[pl.ds(0, spans - 1)]
        pltpu.make_async_copy(slots, slots, sems.at[which]).wait()

    for s in others:
        to_span(ts_ref.at[:, pl.ds(own_start(s), span_len)], ts_rx.at[my_s], 0, s)
    local[0].wait()
    templates = tm_ref[...]
    gr_rx[my_s] = pack(dot_nt(templates, templates))
    for s in others:
        to_span(gr_rx.at[my_s], gr_rx.at[my_s], 1, s)

    for copy in local[2:]:
        copy.wait()

    code = slot_codes(ht_ref[...])
    own_code = jnp.sum(jnp.where(iota(code.shape, 0) == my_s, code, 0.0), axis=0, keepdims=True)
    slots = spans * CAP
    selector = (own_code == iota((slots, hits), 0).astype(F32)).astype(BF16)

    time = (iota((det_w, span_len), 1) + my_s * span_len).astype(F32)
    cut_start = to_column(cs_ref[...])
    cut_end = cut_start + to_column(cl_ref[...])
    inside = (time >= cut_start) & (time < cut_end)
    sw_ref[...] = jnp.where(inside, 0.0, to_column(dw_ref[...])).astype(BF16).astype(F32)

    coarse_count = wafers * hits
    assert max(coarse_count, pix) <= 256
    pair = 2 * ROWS
    nought = jnp.zeros((pair, span_len), BF16)
    unit = jnp.ones((pair, span_len), BF16)

    def numbered(count):
        rows = iota((pair, span_len), 0).astype(F32)
        return [(rows + float(start)).astype(BF16) for start in range(0, count, pair)]

    coarse_iota, fine_iota = numbered(coarse_count), numbered(pix)

    def spread(row):
        return jnp.broadcast_to(row, (pair, span_len)).astype(BF16)

    def one_hot(numbers, index, value):
        index = spread(index)
        return jnp.concatenate([jnp.where(block == index, value, nought) for block in numbers], axis=0)

    def shifted(x, amount):
        return lax.shift_right_logical(x, jnp.full(x.shape, amount, jnp.int32))

    def coarse_of(points):
        coarse = (shifted(points, log2(pix)) & (wafers - 1)) * hits + shifted(points, log2(TILE))
        return coarse.astype(F32)

    groups = det_w // ROWS
    keep_left = left_ref.shape[0] == groups

    def place(coarse, values):
        return jnp.concatenate(
            [
                one_hot(coarse_iota, coarse[r : r + 1, :], spread(values[r : r + 1, :]))
                for r in range(ROWS)
            ],
            axis=1,
        )

    def rows_of(g):
        return pl.ds(g * ROWS if isinstance(g, int) else pl.multiple_of(g * ROWS, ROWS), ROWS)

    def prepare(g, carry):
        points = pt_ref[rows_of(g), :]
        fine = (points & (pix - 1)).astype(F32)
        hot_ref[g] = jnp.concatenate(
            [one_hot(fine_iota, fine[r : r + 1, :], unit) for r in range(ROWS)], axis=1
        )
        if keep_left:
            left_ref[g] = place(coarse_of(points), sw_ref[rows_of(g), :])
        return carry

    lax.fori_loop(0, groups, prepare, 0, unroll=2)

    same_line = (bg_ref[...].astype(F32) == to_column(bg_ref[...])).astype(F32)
    local[1].wait()
    span_wait(ts_rx, span_recv, 0)
    for s in range(spans):
        ts_all[s * det_dev : (s + 1) * det_dev, :] = ts_rx[s]
    stream = ts_all[...]
    cleaned = stream - dot_nn(same_line, stream) * (NGROUP / det_w)
    pj_rx[my_s] = pack(dot_nt(cleaned, templates))
    for s in others:
        to_span(pj_rx.at[my_s], pj_rx.at[my_s], 2, s)

    span_wait(gr_rx, span_recv, 1)
    inverse = inverse_spd(unpack(jnp.sum(gr_rx[...], axis=0)))
    solved = dot_nn(inverse, templates)

    span_wait(pj_rx, span_recv, 2)
    projection = unpack(jnp.sum(pj_rx[...], axis=0))
    filtered = cleaned - dot_nn(projection, solved)
    val_ref[...] = (sw_ref[...] * filtered).astype(BF16).astype(F32)

    def bin_group(g, part):
        coarse = coarse_of(pt_ref[rows_of(g), :])
        weights = left_ref[g] if keep_left else place(coarse, sw_ref[rows_of(g), :])
        left = jnp.concatenate([place(coarse, val_ref[rows_of(g), :]), weights], axis=0)
        return part + lax.dot_general(
            left, hot_ref[g], (((1,), (1,)), ((), ())), preferred_element_type=F32
        )

    part = jnp.zeros((2 * coarse_count, pix), F32)
    if groups <= 8:
        for g in range(groups):
            part = bin_group(g, part)
    else:
        part = lax.fori_loop(0, groups, bin_group, part)

    for q in range(wafers):
        for m in range(2):
            start = (m * wafers + q) * hits
            wafer_tx[q, m * hits : (m + 1) * hits] = part[start : start + hits, :]
    for w in other_wafers:
        pltpu.make_async_remote_copy(
            src_ref=wafer_tx.at[w], dst_ref=wafer_rx.at[my_w],
            send_sem=wafer_send, recv_sem=wafer_recv,
            device_id=(w, my_s), device_id_type=MESH,
        ).start()
    wafer_rx[my_w] = wafer_tx[my_w]
    arrivals, departures = wafer_rx.at[pl.ds(0, wafers - 1)], wafer_tx.at[pl.ds(0, wafers - 1)]
    pltpu.make_async_copy(arrivals, arrivals, wafer_recv).wait()
    shared = jnp.sum(wafer_rx[...], axis=0)
    out = dot_selected(selector, jnp.concatenate([shared[:hits, :], shared[hits:, :]], axis=1))
    for o in range(spans):
        for m in range(2):
            tx[o, m * CAP : (m + 1) * CAP] = out[o * CAP : (o + 1) * CAP, m * pix : (m + 1) * pix]
    for s in others:
        to_span(tx.at[s], rx.at[my_s], 3, s)
    own = pltpu.make_async_copy(tx.at[my_s], rx.at[my_s], local_sem.at[0])
    own.start()

    mine = (iota((det_dev, det_w), 1) == iota((det_dev, det_w), 0) + my_s * det_dev).astype(F32)
    fit_ref[...] = dot_nn(dot_nn(mine, projection), inverse)
    fit = pltpu.make_async_copy(fit_ref, fit_hbm, local_sem.at[1])
    fit.start()
    for which, buffer in enumerate((ts_rx, gr_rx, pj_rx)):
        span_wait(buffer, span_send, which)
    own.wait()
    fit.wait()
    pltpu.make_async_copy(departures, departures, wafer_send).wait()
    span_wait(tx, span_send, 3)
    span_wait(rx, span_recv, 3)


def collect(
    rx_hbm, fit_hbm, ht_hbm, fit_out, rhs_ref, wgt_ref, rx, ht_ref, sems
):
    arrivals = pltpu.make_async_copy(rx_hbm, rx, sems.at[0])
    listing = pltpu.make_async_copy(ht_hbm, ht_ref, sems.at[1])
    fit = pltpu.make_async_copy(fit_hbm, fit_out, sems.at[2])
    listing.start()
    arrivals.start()
    fit.start()
    my_s = lax.axis_index("span")
    pix = rhs_ref.shape[1]
    listing.wait()
    listed = ht_ref[...]
    code = slot_codes(listed)
    place = (listed - (my_s * TILE_OWN - 1)).astype(F32)
    landing = [
        jnp.sum(jnp.where(code == (my_s * CAP + k).astype(F32), place, 0.0), axis=1, keepdims=True) - 1.0
        for k in range(CAP)
    ]
    row_iota = iota((TILE_OWN, pix), 0).astype(F32)
    sums = [jnp.zeros((TILE_OWN, pix), F32) for m in range(2)]
    arrivals.wait()
    for s in range(rx.shape[0]):
        arrived = rx[s]
        for k in range(CAP):
            here = row_iota == landing[k][s : s + 1, :]
            for m in range(2):
                row = m * CAP + k
                sums[m] = sums[m] + jnp.where(here, arrived[row : row + 1, :], 0.0)
    rhs_ref[...] = sums[0]
    wgt_ref[...] = sums[1]
    fit.wait()


def body(timestream, templates, bias_group, det_weight, cut_start, cut_len, pointing, hit_tiles):
    wafers, spans = lax.axis_size("wafer"), lax.axis_size("span")
    det_dev = timestream.shape[0]
    nt, span_len = templates.shape
    det_w = pointing.shape[0]
    pix = TILE // wafers
    vmem = pl.BlockSpec(memory_space=pltpu.VMEM)
    anywhere = pl.BlockSpec(memory_space=pl.ANY)
    fit_shape = jax.ShapeDtypeStruct((det_dev, nt), F32)
    map_shape = jax.ShapeDtypeStruct((TILE_OWN, pix), F32)
    hits = hit_tiles.shape[1]
    groups = det_w // ROWS
    fit, tiles = pl.pallas_call(
        functools.partial(kernel, wafers, spans),
        out_shape=(fit_shape, jax.ShapeDtypeStruct((spans, 2 * CAP, pix), F32)),
        in_specs=[anywhere] * 8,
        out_specs=(anywhere,) * 2,
        scratch_shapes=[
            pltpu.VMEM((nt, span_len), F32),
            pltpu.VMEM((1, det_w), jnp.int32),
            pltpu.VMEM((1, det_w), F32),
            pltpu.VMEM((1, det_w), jnp.int32),
            pltpu.VMEM((1, det_w), jnp.int32),
            pltpu.VMEM((det_w, span_len), jnp.int32),
            pltpu.VMEM(hit_tiles.shape, jnp.int32),
            pltpu.VMEM((spans, det_dev, span_len), F32),
            pltpu.VMEM((det_w, span_len), F32),
            pltpu.VMEM((spans, nt // 2, 2 * nt), F32),
            pltpu.VMEM((spans, det_w // 2, 2 * nt), F32),
            pltpu.VMEM((det_w, span_len), F32),
            pltpu.VMEM((det_w, span_len), F32),
            pltpu.VMEM((groups, pix, ROWS * span_len), BF16),
            pltpu.VMEM((groups if groups <= 8 else 1, wafers * hits, ROWS * span_len), BF16),
            pltpu.VMEM((wafers, 2 * hits, pix), F32),
            pltpu.VMEM((wafers, 2 * hits, pix), F32),
            pltpu.VMEM((spans, 2 * CAP, pix), F32),
            pltpu.VMEM((det_dev, nt), F32),
            pltpu.SemaphoreType.DMA((4,)),
            pltpu.SemaphoreType.DMA((4,)),
            pltpu.SemaphoreType.DMA,
            pltpu.SemaphoreType.DMA,
            pltpu.SemaphoreType.DMA((8,)),
        ],
        compiler_params=pltpu.CompilerParams(
            collective_id=0, has_side_effects=True, vmem_limit_bytes=56 * 1024 * 1024
        ),
    )(
        timestream, templates, bias_group.reshape(1, det_w), det_weight.reshape(1, det_w),
        cut_start.reshape(1, det_w), cut_len.reshape(1, det_w), pointing, hit_tiles,
    )
    return pl.pallas_call(
        collect,
        out_shape=(fit_shape, map_shape, map_shape),
        in_specs=[anywhere] * 3,
        out_specs=(anywhere, vmem, vmem),
        scratch_shapes=[
            pltpu.VMEM((spans, 2 * CAP, pix), F32),
            pltpu.VMEM(hit_tiles.shape, jnp.int32),
            pltpu.SemaphoreType.DMA((3,)),
        ],
    )(tiles, fit, hit_tiles)


def solution(mesh):
    in_specs = (
        P(("wafer", "span"), None),
        P(None, "span"),
        P("wafer"),
        P("wafer"),
        P("wafer"),
        P("wafer"),
        P("wafer", "span"),
        P(),
    )
    out_specs = (P(("wafer", "span"), None), P("span", "wafer"), P("span", "wafer"))
    return jax.shard_map(body, mesh=mesh, in_specs=in_specs, out_specs=out_specs, check_vma=False)
```

```python
import functools

import jax
import jax.numpy as jnp
from jax import lax
from jax.experimental import pallas as pl
from jax.experimental.pallas import tpu as pltpu
from jax.sharding import PartitionSpec as P

NGROUP = 12
TILE = 512
TILE_OWN = 8
CAP = 2
ROWS = 8
HIGHEST = lax.Precision.HIGHEST
MESH = pl.DeviceIdType.MESH
F32 = jnp.float32
BF16 = jnp.bfloat16


def dot_nn(a, b):
    return lax.dot_general(a, b, (((1,), (0,)), ((), ())), precision=HIGHEST, preferred_element_type=F32)


def dot_nt(a, b):
    return lax.dot_general(a, b, (((1,), (1,)), ((), ())), precision=HIGHEST, preferred_element_type=F32)


def dot_tn(a, b):
    return lax.dot_general(a, b, (((0,), (0,)), ((), ())), precision=HIGHEST, preferred_element_type=F32)


def iota(shape, dim):
    return lax.broadcasted_iota(jnp.int32, shape, dim)


def dot_selected(selector, values):
    high = values.astype(BF16)
    rest = values - high.astype(F32)
    middle = rest.astype(BF16)
    low = (rest - middle.astype(F32)).astype(BF16)
    out = [jnp.dot(selector, part, preferred_element_type=F32) for part in (low, middle, high)]
    return (out[0] + out[1]) + out[2]


def to_column(row):
    size = row.shape[1]
    eye = iota((size, size), 0) == iota((size, size), 1)
    return jnp.sum(jnp.where(eye, row.astype(F32), 0.0), axis=1, keepdims=True)


def log2(value):
    assert value & (value - 1) == 0
    return value.bit_length() - 1


def reciprocal(x):
    guess = pl.reciprocal(x, approx=True)
    guess = guess * (2.0 - x * guess)
    return guess * (2.0 - x * guess)


def inverse_spd(gram):
    size = gram.shape[0]
    wide = 2 * size
    eye = (iota((size, size), 0) == iota((size, size), 1)).astype(F32)
    joined = jnp.concatenate([eye, gram], axis=1)
    blocks = [joined[ROWS * b : ROWS * (b + 1), :] for b in range(size // ROWS)]
    row_of = iota((ROWS, wide), 0)
    for p in range(size // ROWS):
        spread = [
            [
                jnp.broadcast_to(block[:, size + p * ROWS + c : size + p * ROWS + c + 1], (ROWS, wide))
                for c in range(ROWS)
            ]
            for block in blocks
        ]
        panel = blocks[p]
        columns = list(spread[p])
        for k in range(ROWS):
            pivot = columns[k]
            here = row_of == k
            scale = reciprocal(jnp.broadcast_to(pivot[k : k + 1, :], (ROWS, wide)))

            def swept(block):
                top = block[k : k + 1, :]
                return jnp.where(here, 0.0, block) - jnp.where(here, -top, pivot * top) * scale

            panel = swept(panel)
            for c in range(k + 1, ROWS):
                columns[c] = swept(columns[c])
        for b in range(len(blocks)):
            if b == p:
                blocks[b] = panel
            else:
                terms = [spread[b][c] * panel[c : c + 1, :] for c in range(ROWS)]
                while len(terms) > 1:
                    terms = [x + y for x, y in zip(terms[::2], terms[1::2])]
                blocks[b] = blocks[b] - terms[0]
    return jnp.concatenate(blocks, axis=0)[:, :size]


def pack(tall):
    half = tall.shape[0] // 2
    return jnp.concatenate([tall[:half, :], tall[half:, :]], axis=1)


def unpack(wide):
    half = wide.shape[1] // 2
    return jnp.concatenate([wide[:, :half], wide[:, half:]], axis=0)


def slot_codes(listed):
    owner = lax.shift_right_logical(listed, jnp.full(listed.shape, log2(TILE_OWN), jnp.int32)).astype(F32)
    lane = iota(listed.shape, 1)
    rank = jnp.zeros(listed.shape, F32)
    for j in range(listed.shape[1] - 1):
        rank += jnp.where((owner[:, j : j + 1] == owner) & (lane > j), 1.0, 0.0)
    return owner * CAP + rank


def kernel(
    wafers, spans,
    ts_ref, tm_hbm, bg_hbm, dw_hbm, cs_hbm, cl_hbm, pt_hbm, ht_hbm,
    fit_hbm, rx, marks_hbm,
    tm_ref, bg_ref, dw_ref, cs_ref, cl_ref, pt_ref, ht_ref,
    ts_rx, ts_all, gr_rx, pj_rx, sw_ref, val_ref, hot_ref, left_ref, wafer_tx, wafer_rx, tx, fit_ref, marks_ref,
    span_send, span_recv, wafer_send, wafer_recv, local_sem,
):
    det_dev = ts_ref.shape[0]
    nt, span_len = tm_ref.shape
    det_w = pt_ref.shape[0]
    hits = ht_ref.shape[1]
    pix = TILE // wafers
    my_w, my_s = lax.axis_index("wafer"), lax.axis_index("span")

    others = [lax.rem(my_s + i, spans) for i in range(1, spans)]
    other_wafers = [lax.rem(my_w + i, wafers) for i in range(1, wafers)]

    def own_start(s):
        return pl.multiple_of(s * span_len, span_len)

    pairs = (
        (tm_hbm, tm_ref),
        (ts_ref.at[:, pl.ds(own_start(my_s), span_len)], ts_rx.at[my_s]),
        (pt_hbm, pt_ref), (cs_hbm, cs_ref), (cl_hbm, cl_ref), (dw_hbm, dw_ref), (ht_hbm, ht_ref), (bg_hbm, bg_ref),
    )
    local = [pltpu.make_async_copy(a, b, local_sem.at[i]) for i, (a, b) in enumerate(pairs)]
    barrier = pltpu.get_barrier_semaphore()
    for s in others:
        pl.semaphore_signal(barrier, inc=1, device_id=(my_w, s), device_id_type=MESH)
    for w in other_wafers:
        pl.semaphore_signal(barrier, inc=1, device_id=(w, my_s), device_id_type=MESH)
    for copy in local:
        copy.start()
    pl.semaphore_wait(barrier, spans + wafers - 2)

    def to_span(src, dst, which, s):
        pltpu.make_async_remote_copy(
            src_ref=src, dst_ref=dst, send_sem=span_send.at[which], recv_sem=span_recv.at[which],
            device_id=(my_w, s), device_id_type=MESH,
        ).start()

    def span_wait(buffer, sems, which):
        slots = buffer.at[pl.ds(0, spans - 1)]
        pltpu.make_async_copy(slots, slots, sems.at[which]).wait()

    for s in others:
        to_span(ts_ref.at[:, pl.ds(own_start(s), span_len)], ts_rx.at[my_s], 0, s)
    local[0].wait()
    templates = tm_ref[...]
    gr_rx[my_s] = pack(dot_nt(templates, templates))
    for s in others:
        to_span(gr_rx.at[my_s], gr_rx.at[my_s], 1, s)

    for copy in local[2:]:
        copy.wait()

    code = slot_codes(ht_ref[...])
    own_code = jnp.sum(jnp.where(iota(code.shape, 0) == my_s, code, 0.0), axis=0, keepdims=True)
    slots = spans * CAP
    selector = (own_code == iota((slots, hits), 0).astype(F32)).astype(BF16)

    place_of = (ht_ref[...] - (my_s * TILE_OWN - 1)).astype(F32)
    for k in range(CAP):
        mine = code == (my_s * CAP + k).astype(F32)
        landing = jnp.sum(jnp.where(mine, place_of, 0.0), axis=1, keepdims=True) - 1.0
        marks_ref[k] = jnp.broadcast_to(landing, (spans, pix))
    marks = pltpu.make_async_copy(marks_ref, marks_hbm, local_sem.at[2])
    marks.start()

    time = (iota((det_w, span_len), 1) + my_s * span_len).astype(F32)
    cut_start = to_column(cs_ref[...])
    cut_end = cut_start + to_column(cl_ref[...])
    inside = (time >= cut_start) & (time < cut_end)
    sw_ref[...] = jnp.where(inside, 0.0, to_column(dw_ref[...])).astype(BF16).astype(F32)

    coarse_count = wafers * hits
    assert max(coarse_count, pix) <= 256
    pair = 2 * ROWS
    nought = jnp.zeros((pair, span_len), BF16)
    unit = jnp.ones((pair, span_len), BF16)

    def numbered(count):
        rows = iota((pair, span_len), 0).astype(F32)
        return [(rows + float(start)).astype(BF16) for start in range(0, count, pair)]

    coarse_iota, fine_iota = numbered(coarse_count), numbered(pix)

    def spread(row):
        return jnp.broadcast_to(row, (pair, span_len)).astype(BF16)

    def one_hot(numbers, index, value):
        index = spread(index)
        return jnp.concatenate([jnp.where(block == index, value, nought) for block in numbers], axis=0)

    def shifted(x, amount):
        return lax.shift_right_logical(x, jnp.full(x.shape, amount, jnp.int32))

    def coarse_of(points):
        coarse = (shifted(points, log2(pix)) & (wafers - 1)) * hits + shifted(points, log2(TILE))
        return coarse.astype(F32)

    groups = det_w // ROWS
    keep_left = left_ref.shape[0] == groups

    def place(coarse, values):
        return jnp.concatenate(
            [
                one_hot(coarse_iota, coarse[r : r + 1, :], spread(values[r : r + 1, :]))
                for r in range(ROWS)
            ],
            axis=1,
        )

    def rows_of(g):
        return pl.ds(g * ROWS if isinstance(g, int) else pl.multiple_of(g * ROWS, ROWS), ROWS)

    def prepare(g, carry):
        points = pt_ref[rows_of(g), :]
        fine = (points & (pix - 1)).astype(F32)
        hot_ref[g] = jnp.concatenate(
            [one_hot(fine_iota, fine[r : r + 1, :], unit) for r in range(ROWS)], axis=1
        )
        if keep_left:
            left_ref[g] = place(coarse_of(points), sw_ref[rows_of(g), :])
        return carry

    lax.fori_loop(0, groups, prepare, 0, unroll=2)

    same_line = (bg_ref[...].astype(F32) == to_column(bg_ref[...])).astype(BF16)
    local[1].wait()
    span_wait(ts_rx, span_recv, 0)
    for s in range(spans):
        ts_all[s * det_dev : (s + 1) * det_dev, :] = ts_rx[s]
    stream = ts_all[...]
    cleaned = stream - dot_selected(same_line, stream) * (NGROUP / det_w)
    pj_rx[my_s] = pack(dot_nt(cleaned, templates))
    for s in others:
        to_span(pj_rx.at[my_s], pj_rx.at[my_s], 2, s)

    span_wait(gr_rx, span_recv, 1)
    inverse = inverse_spd(unpack(jnp.sum(gr_rx[...], axis=0)))
    solved = dot_nn(inverse, templates)

    span_wait(pj_rx, span_recv, 2)
    projection = unpack(jnp.sum(pj_rx[...], axis=0))
    filtered = cleaned - dot_nn(projection, solved)
    val_ref[...] = (sw_ref[...] * filtered).astype(BF16).astype(F32)

    def bin_group(g, part):
        coarse = coarse_of(pt_ref[rows_of(g), :])
        weights = left_ref[g] if keep_left else place(coarse, sw_ref[rows_of(g), :])
        left = jnp.concatenate([place(coarse, val_ref[rows_of(g), :]), weights], axis=0)
        return part + lax.dot_general(
            left, hot_ref[g], (((1,), (1,)), ((), ())), preferred_element_type=F32
        )

    part = jnp.zeros((2 * coarse_count, pix), F32)
    if groups <= 8:
        for g in range(groups):
            part = bin_group(g, part)
    else:
        part = lax.fori_loop(0, groups, bin_group, part)

    for q in range(wafers):
        for m in range(2):
            start = (m * wafers + q) * hits
            wafer_tx[q, m * hits : (m + 1) * hits] = part[start : start + hits, :]
    for w in other_wafers:
        pltpu.make_async_remote_copy(
            src_ref=wafer_tx.at[w], dst_ref=wafer_rx.at[my_w],
            send_sem=wafer_send, recv_sem=wafer_recv,
            device_id=(w, my_s), device_id_type=MESH,
        ).start()
    wafer_rx[my_w] = wafer_tx[my_w]
    arrivals, departures = wafer_rx.at[pl.ds(0, wafers - 1)], wafer_tx.at[pl.ds(0, wafers - 1)]
    pltpu.make_async_copy(arrivals, arrivals, wafer_recv).wait()
    shared = jnp.sum(wafer_rx[...], axis=0)
    out = dot_selected(selector, jnp.concatenate([shared[:hits, :], shared[hits:, :]], axis=1))
    for o in range(spans):
        for m in range(2):
            tx[o, m * CAP : (m + 1) * CAP] = out[o * CAP : (o + 1) * CAP, m * pix : (m + 1) * pix]
    for s in others:
        to_span(tx.at[s], rx.at[my_s], 3, s)
    own = pltpu.make_async_copy(tx.at[my_s], rx.at[my_s], local_sem.at[0])
    own.start()

    mine = (iota((det_dev, det_w), 1) == iota((det_dev, det_w), 0) + my_s * det_dev).astype(F32)
    fit_ref[...] = dot_nn(dot_nn(mine, projection), inverse)
    fit = pltpu.make_async_copy(fit_ref, fit_hbm, local_sem.at[1])
    fit.start()
    for which, buffer in enumerate((ts_rx, gr_rx, pj_rx)):
        span_wait(buffer, span_send, which)
    own.wait()
    fit.wait()
    marks.wait()
    pltpu.make_async_copy(departures, departures, wafer_send).wait()
    span_wait(tx, span_send, 3)
    span_wait(rx, span_recv, 3)


def collect(rx_hbm, fit_hbm, marks_hbm, fit_out, rhs_ref, wgt_ref, rx, marks_ref, sems):
    arrivals = pltpu.make_async_copy(rx_hbm, rx, sems.at[0])
    marks = pltpu.make_async_copy(marks_hbm, marks_ref, sems.at[1])
    fit = pltpu.make_async_copy(fit_hbm, fit_out, sems.at[2])
    marks.start()
    arrivals.start()
    fit.start()
    row_iota = iota(rhs_ref.shape, 0).astype(F32)
    sums = [jnp.zeros(rhs_ref.shape, F32) for m in range(2)]
    marks.wait()
    arrivals.wait()
    for s in range(rx.shape[0]):
        arrived = rx[s]
        for k in range(CAP):
            here = row_iota == marks_ref[k, s : s + 1, :]
            for m in range(2):
                row = m * CAP + k
                sums[m] = sums[m] + jnp.where(here, arrived[row : row + 1, :], 0.0)
    rhs_ref[...] = sums[0]
    wgt_ref[...] = sums[1]
    fit.wait()


def body(timestream, templates, bias_group, det_weight, cut_start, cut_len, pointing, hit_tiles):
    wafers, spans = lax.axis_size("wafer"), lax.axis_size("span")
    det_dev = timestream.shape[0]
    nt, span_len = templates.shape
    det_w = pointing.shape[0]
    pix = TILE // wafers
    vmem = pl.BlockSpec(memory_space=pltpu.VMEM)
    anywhere = pl.BlockSpec(memory_space=pl.ANY)
    fit_shape = jax.ShapeDtypeStruct((det_dev, nt), F32)
    map_shape = jax.ShapeDtypeStruct((TILE_OWN, pix), F32)
    hits = hit_tiles.shape[1]
    groups = det_w // ROWS
    marks_shape = (CAP, spans, pix)
    fit, tiles, marks = pl.pallas_call(
        functools.partial(kernel, wafers, spans),
        out_shape=(fit_shape, jax.ShapeDtypeStruct((spans, 2 * CAP, pix), F32), jax.ShapeDtypeStruct(marks_shape, F32)),
        in_specs=[anywhere] * 8,
        out_specs=(anywhere,) * 3,
        scratch_shapes=[
            pltpu.VMEM((nt, span_len), F32),
            pltpu.VMEM((1, det_w), jnp.int32),
            pltpu.VMEM((1, det_w), F32),
            pltpu.VMEM((1, det_w), jnp.int32),
            pltpu.VMEM((1, det_w), jnp.int32),
            pltpu.VMEM((det_w, span_len), jnp.int32),
            pltpu.VMEM(hit_tiles.shape, jnp.int32),
            pltpu.VMEM((spans, det_dev, span_len), F32),
            pltpu.VMEM((det_w, span_len), F32),
            pltpu.VMEM((spans, nt // 2, 2 * nt), F32),
            pltpu.VMEM((spans, det_w // 2, 2 * nt), F32),
            pltpu.VMEM((det_w, span_len), F32),
            pltpu.VMEM((det_w, span_len), F32),
            pltpu.VMEM((groups, pix, ROWS * span_len), BF16),
            pltpu.VMEM((groups if groups <= 8 else 1, wafers * hits, ROWS * span_len), BF16),
            pltpu.VMEM((wafers, 2 * hits, pix), F32),
            pltpu.VMEM((wafers, 2 * hits, pix), F32),
            pltpu.VMEM((spans, 2 * CAP, pix), F32),
            pltpu.VMEM((det_dev, nt), F32),
            pltpu.VMEM(marks_shape, F32),
            pltpu.SemaphoreType.DMA((4,)),
            pltpu.SemaphoreType.DMA((4,)),
            pltpu.SemaphoreType.DMA,
            pltpu.SemaphoreType.DMA,
            pltpu.SemaphoreType.DMA((8,)),
        ],
        compiler_params=pltpu.CompilerParams(
            collective_id=0, has_side_effects=True, vmem_limit_bytes=56 * 1024 * 1024
        ),
    )(
        timestream, templates, bias_group.reshape(1, det_w), det_weight.reshape(1, det_w),
        cut_start.reshape(1, det_w), cut_len.reshape(1, det_w), pointing, hit_tiles,
    )
    return pl.pallas_call(
        collect,
        out_shape=(fit_shape, map_shape, map_shape),
        in_specs=[anywhere] * 3,
        out_specs=(anywhere, vmem, vmem),
        scratch_shapes=[
            pltpu.VMEM((spans, 2 * CAP, pix), F32),
            pltpu.VMEM(marks_shape, F32),
            pltpu.SemaphoreType.DMA((3,)),
        ],
    )(tiles, fit, marks)


def solution(mesh):
    in_specs = (
        P(("wafer", "span"), None),
        P(None, "span"),
        P("wafer"),
        P("wafer"),
        P("wafer"),
        P("wafer"),
        P("wafer", "span"),
        P(),
    )
    out_specs = (P(("wafer", "span"), None), P("span", "wafer"), P("span", "wafer"))
    return jax.shard_map(body, mesh=mesh, in_specs=in_specs, out_specs=out_specs, check_vma=False)
```

```python
import functools

import jax
import jax.numpy as jnp
from jax import lax
from jax.experimental import pallas as pl
from jax.experimental.pallas import tpu as pltpu
from jax.sharding import PartitionSpec as P

NGROUP = 12
TILE = 512
TILE_OWN = 8
CAP = 2
ROWS = 8
HIGHEST = lax.Precision.HIGHEST
MESH = pl.DeviceIdType.MESH
F32 = jnp.float32
BF16 = jnp.bfloat16


def dot_nn(a, b):
    return lax.dot_general(a, b, (((1,), (0,)), ((), ())), precision=HIGHEST, preferred_element_type=F32)


def dot_nt(a, b):
    return lax.dot_general(a, b, (((1,), (1,)), ((), ())), precision=HIGHEST, preferred_element_type=F32)


def dot_tn(a, b):
    return lax.dot_general(a, b, (((0,), (0,)), ((), ())), precision=HIGHEST, preferred_element_type=F32)


def iota(shape, dim):
    return lax.broadcasted_iota(jnp.int32, shape, dim)


def dot_selected(selector, values):
    high = values.astype(BF16)
    rest = values - high.astype(F32)
    middle = rest.astype(BF16)
    low = (rest - middle.astype(F32)).astype(BF16)
    out = [jnp.dot(selector, part, preferred_element_type=F32) for part in (low, middle, high)]
    return (out[0] + out[1]) + out[2]


def to_column(row):
    size = row.shape[1]
    eye = iota((size, size), 0) == iota((size, size), 1)
    return jnp.sum(jnp.where(eye, row.astype(F32), 0.0), axis=1, keepdims=True)


def log2(value):
    assert value & (value - 1) == 0
    return value.bit_length() - 1


def inverse_spd(gram):
    size = gram.shape[0]
    wide = 2 * size
    eye = (iota((size, size), 0) == iota((size, size), 1)).astype(F32)
    joined = jnp.concatenate([eye, gram], axis=1)
    blocks = [joined[ROWS * b : ROWS * (b + 1), :] for b in range(size // ROWS)]
    row_of = iota((ROWS, wide), 0)
    for p in range(size // ROWS):
        spread = [
            [
                jnp.broadcast_to(block[:, size + p * ROWS + c : size + p * ROWS + c + 1], (ROWS, wide))
                for c in range(ROWS)
            ]
            for block in blocks
        ]
        panel = blocks[p]
        columns = list(spread[p])
        for k in range(ROWS):
            pivot = columns[k]
            scale = 1.0 / pivot[k : k + 1, :]
            here = row_of == k
            top = panel[k : k + 1, :] * scale
            panel = jnp.where(here, top, panel - pivot * top)
            for c in range(k + 1, ROWS):
                top = columns[c][k : k + 1, :] * scale
                columns[c] = jnp.where(here, top, columns[c] - pivot * top)
        for b in range(len(blocks)):
            if b == p:
                blocks[b] = panel
            else:
                terms = [spread[b][c] * panel[c : c + 1, :] for c in range(ROWS)]
                while len(terms) > 1:
                    terms = [x + y for x, y in zip(terms[::2], terms[1::2])]
                blocks[b] = blocks[b] - terms[0]
    return jnp.concatenate(blocks, axis=0)[:, :size]


def pack(tall):
    half = tall.shape[0] // 2
    return jnp.concatenate([tall[:half, :], tall[half:, :]], axis=1)


def unpack(wide):
    half = wide.shape[1] // 2
    return jnp.concatenate([wide[:, :half], wide[:, half:]], axis=0)


def slot_codes(listed):
    owner = lax.shift_right_logical(listed, jnp.full(listed.shape, log2(TILE_OWN), jnp.int32)).astype(F32)
    lane = iota(listed.shape, 1)
    rank = jnp.zeros(listed.shape, F32)
    for j in range(listed.shape[1] - 1):
        rank += jnp.where((owner[:, j : j + 1] == owner) & (lane > j), 1.0, 0.0)
    return owner * CAP + rank


def kernel(
    wafers, spans,
    ts_ref, tm_hbm, bg_hbm, dw_hbm, cs_hbm, cl_hbm, pt_hbm, ht_hbm,
    fit_hbm, rx,
    tm_ref, bg_ref, dw_ref, cs_ref, cl_ref, pt_ref, ht_ref,
    ts_rx, ts_all, gr_rx, pj_rx, sw_ref, val_ref, hot_ref, left_ref, tx, fit_ref,
    span_send, span_recv, wafer_send, wafer_recv, local_sem,
):
    det_dev = ts_ref.shape[0]
    nt, span_len = tm_ref.shape
    det_w = pt_ref.shape[0]
    hits = ht_ref.shape[1]
    pix = TILE // wafers
    my_w, my_s = lax.axis_index("wafer"), lax.axis_index("span")

    others = [lax.rem(my_s + i, spans) for i in range(1, spans)]
    other_wafers = [lax.rem(my_w + i, wafers) for i in range(1, wafers)]

    def own_start(s):
        return pl.multiple_of(s * span_len, span_len)

    pairs = (
        (tm_hbm, tm_ref),
        (ts_ref.at[:, pl.ds(own_start(my_s), span_len)], ts_rx.at[my_s]),
        (pt_hbm, pt_ref), (cs_hbm, cs_ref), (cl_hbm, cl_ref), (dw_hbm, dw_ref), (ht_hbm, ht_ref), (bg_hbm, bg_ref),
    )
    local = [pltpu.make_async_copy(a, b, local_sem.at[i]) for i, (a, b) in enumerate(pairs)]
    barrier = pltpu.get_barrier_semaphore()
    for s in others:
        pl.semaphore_signal(barrier, inc=1, device_id=(my_w, s), device_id_type=MESH)
    for w in other_wafers:
        pl.semaphore_signal(barrier, inc=1, device_id=(w, my_s), device_id_type=MESH)
    for copy in local:
        copy.start()
    pl.semaphore_wait(barrier, spans + wafers - 2)

    def to_span(src, dst, which, s):
        pltpu.make_async_remote_copy(
            src_ref=src, dst_ref=dst, send_sem=span_send.at[which], recv_sem=span_recv.at[which],
            device_id=(my_w, s), device_id_type=MESH,
        ).start()

    def span_wait(buffer, sems, which):
        slots = buffer.at[pl.ds(0, spans - 1)]
        pltpu.make_async_copy(slots, slots, sems.at[which]).wait()

    for s in others:
        to_span(ts_ref.at[:, pl.ds(own_start(s), span_len)], ts_rx.at[my_s], 0, s)
    local[0].wait()
    templates = tm_ref[...]
    gr_rx[my_s] = pack(dot_nt(templates, templates))
    for s in others:
        to_span(gr_rx.at[my_s], gr_rx.at[my_s], 1, s)

    for copy in local[2:]:
        copy.wait()

    code = slot_codes(ht_ref[...])
    own_code = jnp.sum(jnp.where(iota(code.shape, 0) == my_s, code, 0.0), axis=0, keepdims=True)
    slots = spans * CAP
    selector = (own_code == iota((slots, hits), 0).astype(F32)).astype(BF16)

    time = (iota((det_w, span_len), 1) + my_s * span_len).astype(F32)
    cut_start = to_column(cs_ref[...])
    cut_end = cut_start + to_column(cl_ref[...])
    inside = (time >= cut_start) & (time < cut_end)
    sw_ref[...] = jnp.where(inside, 0.0, to_column(dw_ref[...])).astype(BF16).astype(F32)

    coarse_count = wafers * hits
    assert max(coarse_count, pix) <= 256
    pair = 2 * ROWS
    nought = jnp.zeros((pair, span_len), BF16)
    unit = jnp.ones((pair, span_len), BF16)

    def numbered(count):
        rows = iota((pair, span_len), 0).astype(F32)
        return [(rows + float(start)).astype(BF16) for start in range(0, count, pair)]

    coarse_iota, fine_iota = numbered(coarse_count), numbered(pix)

    def spread(row):
        return jnp.broadcast_to(row, (pair, span_len)).astype(BF16)

    def one_hot(numbers, index, value):
        index = spread(index)
        return jnp.concatenate([jnp.where(block == index, value, nought) for block in numbers], axis=0)

    def shifted(x, amount):
        return lax.shift_right_logical(x, jnp.full(x.shape, amount, jnp.int32))

    def coarse_of(points):
        coarse = (shifted(points, log2(pix)) & (wafers - 1)) * hits + shifted(points, log2(TILE))
        return coarse.astype(F32)

    groups = det_w // ROWS
    keep_left = left_ref.shape[0] == groups

    def place(coarse, values):
        return jnp.concatenate(
            [
                one_hot(coarse_iota, coarse[r : r + 1, :], spread(values[r : r + 1, :]))
                for r in range(ROWS)
            ],
            axis=1,
        )

    def rows_of(g):
        return pl.ds(g * ROWS if isinstance(g, int) else pl.multiple_of(g * ROWS, ROWS), ROWS)

    def prepare(g, carry):
        points = pt_ref[rows_of(g), :]
        fine = (points & (pix - 1)).astype(F32)
        hot_ref[g] = jnp.concatenate(
            [one_hot(fine_iota, fine[r : r + 1, :], unit) for r in range(ROWS)], axis=1
        )
        if keep_left:
            left_ref[g] = place(coarse_of(points), sw_ref[rows_of(g), :])
        return carry

    lax.fori_loop(0, groups, prepare, 0, unroll=2)

    same_line = (bg_ref[...].astype(F32) == to_column(bg_ref[...])).astype(F32)
    local[1].wait()
    span_wait(ts_rx, span_recv, 0)
    for s in range(spans):
        ts_all[s * det_dev : (s + 1) * det_dev, :] = ts_rx[s]
    stream = ts_all[...]
    cleaned = stream - dot_nn(same_line, stream) * (NGROUP / det_w)
    pj_rx[my_s] = pack(dot_nt(cleaned, templates))
    for s in others:
        to_span(pj_rx.at[my_s], pj_rx.at[my_s], 2, s)

    span_wait(gr_rx, span_recv, 1)
    inverse = inverse_spd(unpack(jnp.sum(gr_rx[...], axis=0)))
    solved = dot_nn(inverse, templates)

    span_wait(pj_rx, span_recv, 2)
    projection = unpack(jnp.sum(pj_rx[...], axis=0))
    filtered = cleaned - dot_nn(projection, solved)
    val_ref[...] = (sw_ref[...] * filtered).astype(BF16).astype(F32)

    def bin_group(g, part):
        coarse = coarse_of(pt_ref[rows_of(g), :])
        weights = left_ref[g] if keep_left else place(coarse, sw_ref[rows_of(g), :])
        left = jnp.concatenate([place(coarse, val_ref[rows_of(g), :]), weights], axis=0)
        return part + lax.dot_general(
            left, hot_ref[g], (((1,), (1,)), ((), ())), preferred_element_type=F32
        )

    part = jnp.zeros((2 * coarse_count, pix), F32)
    if groups <= 8:
        for g in range(groups):
            part = bin_group(g, part)
    else:
        part = lax.fori_loop(0, groups, bin_group, part)

    wide = jnp.concatenate([part[q * hits : (q + 1) * hits, :] for q in range(2 * wafers)], axis=1)
    out = dot_selected(selector, wide)
    for q in range(wafers):
        for o in range(spans):
            for m in range(2):
                start = (m * wafers + q) * pix
                tx[q * spans + o, m * CAP : (m + 1) * CAP] = out[
                    o * CAP : (o + 1) * CAP, start : start + pix
                ]
    me = my_w * spans + my_s
    for w in other_wafers + [my_w]:
        for s in others + [my_s]:
            if w is my_w and s is my_s:
                continue
            pltpu.make_async_remote_copy(
                src_ref=tx.at[w * spans + s], dst_ref=rx.at[me],
                send_sem=wafer_send, recv_sem=wafer_recv,
                device_id=(w, s), device_id_type=MESH,
            ).start()
    own = pltpu.make_async_copy(tx.at[me], rx.at[me], local_sem.at[0])
    own.start()

    mine = (iota((det_dev, det_w), 1) == iota((det_dev, det_w), 0) + my_s * det_dev).astype(F32)
    fit_ref[...] = dot_nn(dot_nn(mine, projection), inverse)
    fit = pltpu.make_async_copy(fit_ref, fit_hbm, local_sem.at[1])
    fit.start()
    for which, buffer in enumerate((ts_rx, gr_rx, pj_rx)):
        span_wait(buffer, span_send, which)
    own.wait()
    fit.wait()
    total = wafers * spans
    arrivals, departures = rx.at[pl.ds(0, total - 1)], tx.at[pl.ds(0, total - 1)]
    pltpu.make_async_copy(departures, departures, wafer_send).wait()
    pltpu.make_async_copy(arrivals, arrivals, wafer_recv).wait()


def collect(
    rx_hbm, fit_hbm, ht_hbm, fit_out, rhs_ref, wgt_ref, rx, ht_ref, sems
):
    arrivals = pltpu.make_async_copy(rx_hbm, rx, sems.at[0])
    listing = pltpu.make_async_copy(ht_hbm, ht_ref, sems.at[1])
    fit = pltpu.make_async_copy(fit_hbm, fit_out, sems.at[2])
    listing.start()
    arrivals.start()
    fit.start()
    my_s = lax.axis_index("span")
    pix = rhs_ref.shape[1]
    listing.wait()
    listed = ht_ref[...]
    code = slot_codes(listed)
    place = (listed - (my_s * TILE_OWN - 1)).astype(F32)
    landing = [
        jnp.sum(jnp.where(code == (my_s * CAP + k).astype(F32), place, 0.0), axis=1, keepdims=True) - 1.0
        for k in range(CAP)
    ]
    row_iota = iota((TILE_OWN, pix), 0).astype(F32)
    sums = [jnp.zeros((TILE_OWN, pix), F32) for m in range(2)]
    arrivals.wait()
    spans = ht_ref.shape[0]
    for s in range(spans):
        arrived = rx[s]
        for w in range(1, rx.shape[0] // spans):
            arrived = arrived + rx[w * spans + s]
        for k in range(CAP):
            here = row_iota == landing[k][s : s + 1, :]
            for m in range(2):
                row = m * CAP + k
                sums[m] = sums[m] + jnp.where(here, arrived[row : row + 1, :], 0.0)
    rhs_ref[...] = sums[0]
    wgt_ref[...] = sums[1]
    fit.wait()


def body(timestream, templates, bias_group, det_weight, cut_start, cut_len, pointing, hit_tiles):
    wafers, spans = lax.axis_size("wafer"), lax.axis_size("span")
    det_dev = timestream.shape[0]
    nt, span_len = templates.shape
    det_w = pointing.shape[0]
    pix = TILE // wafers
    vmem = pl.BlockSpec(memory_space=pltpu.VMEM)
    anywhere = pl.BlockSpec(memory_space=pl.ANY)
    fit_shape = jax.ShapeDtypeStruct((det_dev, nt), F32)
    map_shape = jax.ShapeDtypeStruct((TILE_OWN, pix), F32)
    hits = hit_tiles.shape[1]
    groups = det_w // ROWS
    fit, tiles = pl.pallas_call(
        functools.partial(kernel, wafers, spans),
        out_shape=(fit_shape, jax.ShapeDtypeStruct((wafers * spans, 2 * CAP, pix), F32)),
        in_specs=[anywhere] * 8,
        out_specs=(anywhere,) * 2,
        scratch_shapes=[
            pltpu.VMEM((nt, span_len), F32),
            pltpu.VMEM((1, det_w), jnp.int32),
            pltpu.VMEM((1, det_w), F32),
            pltpu.VMEM((1, det_w), jnp.int32),
            pltpu.VMEM((1, det_w), jnp.int32),
            pltpu.VMEM((det_w, span_len), jnp.int32),
            pltpu.VMEM(hit_tiles.shape, jnp.int32),
            pltpu.VMEM((spans, det_dev, span_len), F32),
            pltpu.VMEM((det_w, span_len), F32),
            pltpu.VMEM((spans, nt // 2, 2 * nt), F32),
            pltpu.VMEM((spans, det_w // 2, 2 * nt), F32),
            pltpu.VMEM((det_w, span_len), F32),
            pltpu.VMEM((det_w, span_len), F32),
            pltpu.VMEM((groups, pix, ROWS * span_len), BF16),
            pltpu.VMEM((groups if groups <= 8 else 1, wafers * hits, ROWS * span_len), BF16),
            pltpu.VMEM((wafers * spans, 2 * CAP, pix), F32),
            pltpu.VMEM((det_dev, nt), F32),
            pltpu.SemaphoreType.DMA((4,)),
            pltpu.SemaphoreType.DMA((4,)),
            pltpu.SemaphoreType.DMA,
            pltpu.SemaphoreType.DMA,
            pltpu.SemaphoreType.DMA((8,)),
        ],
        compiler_params=pltpu.CompilerParams(
            collective_id=0, has_side_effects=True, vmem_limit_bytes=56 * 1024 * 1024
        ),
    )(
        timestream, templates, bias_group.reshape(1, det_w), det_weight.reshape(1, det_w),
        cut_start.reshape(1, det_w), cut_len.reshape(1, det_w), pointing, hit_tiles,
    )
    return pl.pallas_call(
        collect,
        out_shape=(fit_shape, map_shape, map_shape),
        in_specs=[anywhere] * 3,
        out_specs=(anywhere, vmem, vmem),
        scratch_shapes=[
            pltpu.VMEM((wafers * spans, 2 * CAP, pix), F32),
            pltpu.VMEM(hit_tiles.shape, jnp.int32),
            pltpu.SemaphoreType.DMA((3,)),
        ],
    )(tiles, fit, hit_tiles)


def solution(mesh):
    in_specs = (
        P(("wafer", "span"), None),
        P(None, "span"),
        P("wafer"),
        P("wafer"),
        P("wafer"),
        P("wafer"),
        P("wafer", "span"),
        P(),
    )
    out_specs = (P(("wafer", "span"), None), P("span", "wafer"), P("span", "wafer"))
    return jax.shard_map(body, mesh=mesh, in_specs=in_specs, out_specs=out_specs, check_vma=False)
```
